512 devices in a mesh: gx: 16 (over z_lo, core), gy: 8 (over y, z_hi), gz: 4 (over x).
Axes of the slice: x: 4, y: 4, z: 16 (z_hi: 2, z_lo: 8; z = z_hi * 8 + z_lo), core: 2. Of those that a mesh axis runs over, the one named last changes fastest.
Arguments:
- populations: float32 [27, 64, 64, 512], P(None, 'gx', 'gy', 'gz'), may hold values from 0.85 to 1.15
- coarse_populations: float32 [27, 128, 32, 256], P(None, 'gx', 'gy', 'gz'), may hold values from 0.85 to 1.15
- fluid_mask: int32 [64, 64, 512], P('gx', 'gy', 'gz'), may hold values 0 or 1
- inflow: float32 [32, 256], P('gy', 'gz'), may hold values from 0.02 to 0.08
- part_dest: int32 [16, 8, 4, 256, 1], P('gx', 'gy', 'gz'), may hold values from 0 to 15; in each aligned block of 256 rows (0 to 255, 256 to 511, ..., all dimensions but the last counted through in order) at most 32 rows name the same one
- part_cell: int32 [16, 8, 4, 256], P('gx', 'gy', 'gz'), may hold values from 0 to 2942, as said below
- part_vel: float32 [16, 8, 4, 3, 256], P('gx', 'gy', 'gz'), may hold values from -0.3 to 0.3
- part_frac: float32 [16, 8, 4, 3, 256], P('gx', 'gy', 'gz'), may hold values from 0 to 1
- part_drag: float32 [16, 8, 4, 256], P('gx', 'gy', 'gz'), may hold values from 0.05 to 0.5
Outputs:
- fine_next: float32 [27, 64, 64, 512], P(None, 'gx', 'gy', 'gz')
- coarse_next: float32 [27, 128, 32, 256], P(None, 'gx', 'gy', 'gz')
The draws below stay inside these ranges and needn't reach their ends.
Inputs may be any that keep to these rules, and one draw needn't show every extreme that they name: `part_dest`: among the particles of one device at most 32 have the same destination. `part_cell`: ix < 3, iy < 7 and iz < 127, so that all eight corners lie in the destination block.
All inputs are finite; a program needn't handle non-finite values. No bound on the sum of `fluid_mask` on one device may be relied on, other than what follows from the above.
Results may differ from the reference program's by a relative error of at most 0.000078.
Values sent between devices are 32-bit elements; how exact they have to be, the bound alone decides.
No kernel may reach another device: no remote copies, remote signals or barrier semaphores. Data moves between devices by JAX's collectives and lax.ppermute only.
A program may use at most 128 MiB of HBM per device.

```python
import math
import jax
import jax.numpy as jnp
import numpy as np
from jax import lax

CX = 4
CY = 8
CZ = 128
P_DEV = 256
CAP = 32
NX = 64
NY = 64
NZ = 512
LX = 128
N_GX = 16
N_GY = 8
N_GZ = 4


def draw_part_cell(key, part):
    keys = jax.random.split(jax.random.fold_in(key, 7), 3)
    shape = (N_GX, N_GY, N_GZ, P_DEV)
    cell_x = jax.random.randint(keys[0], shape, 0, CX - 1)
    cell_y = jax.random.randint(keys[1], shape, 0, CY - 1)
    cell_z = jax.random.randint(keys[2], shape, 0, CZ - 1)
    return (cell_x * CY * CZ + cell_y * CZ + cell_z).astype(jnp.int32)


def with_ends(entries, key, least, largest):
    longest = entries.shape.index(max(entries.shape))
    spots = []
    for shift in (0, 1):
        where = [jax.random.randint(jax.random.fold_in(key, axis), (), 0, length) for axis, length in enumerate(entries.shape)]
        where[longest] = (where[longest] + shift) % entries.shape[longest]
        spots.append(tuple(where))
    return entries.at[spots[0]].set(least).at[spots[1]].set(largest)


def shard_levels(rng, shape, cuts, low, high):
    gain = 1.0
    for position, parts in cuts:
        steps = jax.random.uniform(jax.random.fold_in(jax.random.fold_in(rng, 6), position), (parts,), jnp.float32, low / len(cuts), high / len(cuts))
        gain = gain * jnp.repeat(jnp.exp(steps), shape[position] // parts).reshape((-1,) + (1,) * (len(shape) - 1 - position))
    return gain


def routed_block(rng, own, number, rows, number_of, top, most, slope):
    ranking = jax.random.permutation(rng, number_of)
    heavy_load, ordinary = shares(number_of, rows * top, most, slope, True), shares(number_of, rows * top, most, slope, False)
    places = jnp.arange(number_of)

    def named(tallies, turn):
        used = int((tallies > 0).sum())
        fixed = max(1, used // 4)
        shifted = fixed + (places - fixed + turn * (used - fixed)) % max(1, number_of - fixed)
        return jnp.zeros((number_of,), jnp.int32).at[ranking[jnp.where(places < fixed, places, shifted)]].set(jnp.asarray(tallies, jnp.int32))

    tallies = jnp.where(number % 4 == 0, named(heavy_load, number // 4), named(ordinary, number - number // 4 - 1))
    mixed = jax.random.permutation(jax.random.fold_in(own, 3), number_of)
    giver, taker = mixed[0:number_of // 2 * 2:2], mixed[1:number_of // 2 * 2:2]
    margin = jnp.minimum(tallies[giver] - 1, most - tallies[taker]) // 2
    margin = jnp.where((giver == ranking[0]) | (taker == ranking[0]) | (tallies[taker] == 0), 0, jnp.maximum(margin, 0))
    shifted = jax.random.randint(jax.random.fold_in(own, 4), (number_of // 2,), 0, 1 << 20) % (margin + 1)
    tallies = tallies.at[giver].add(-shifted).at[taker].add(shifted)
    members = jnp.searchsorted(jnp.cumsum(tallies), jnp.arange(rows * top), side="right").astype(jnp.int32)
    table = members.reshape(top, rows).T
    table = table[jax.random.permutation(jax.random.fold_in(own, 1), rows)]
    turn = jax.random.randint(jax.random.fold_in(own, 2), (rows, 1), 0, top)
    return jnp.take_along_axis(table, (jnp.arange(top)[None, :] + turn) % top, axis=1)


def shares(amount, total, bound, slope, full):
    loads = [(1 << 20) // math.isqrt(standing ** slope) + 1 for standing in range(1, amount + 1)]
    largest = bound if full else min(bound, max(-(-total // amount), total * loads[0] // sum(loads)))
    least = 1 if total - largest >= amount - 1 else 0
    counts, spare = [largest] + [least] * (amount - 1), total - largest - least * (amount - 1)
    while spare > 0:
        free = [i for i in range(1, amount) if counts[i] < largest] or [i for i in range(1, amount) if counts[i] < bound]
        whole, remaining = sum([loads[i] for i in free]), spare
        for i in free:
            more = min(bound - counts[i], max(1, remaining * loads[i] // whole), spare)
            counts[i] = counts[i] + more
            spare = spare - more
    return np.array(counts)


def noise(stream_key, shape, spread, reach, cuts=(), kind=jnp.bfloat16):
    gain = shard_levels(stream_key, shape, cuts, -0.22, 0.18) if cuts else 1.0
    values = jax.random.normal(stream_key, shape, jnp.float32) * spread * gain
    return jnp.minimum(jnp.maximum(values, -reach), reach).astype(kind)


def setup_inputs(seed: int = 0) -> dict:
    splits = jax.random.split(jax.random.key(seed), 10)
    populations = jnp.clip(0.85 + 0.29999995 * jax.random.uniform(splits[0], (27, NX, NY, NZ), jnp.float32) ** shard_levels(splits[0], (27, NX, NY, NZ), ((1, 16), (2, 8), (3, 4)), -0.2, 0.2), 0.85, 1.15)
    coarse_populations = jnp.clip(0.85 + 0.29999995 * jax.random.uniform(splits[1], (27, LX, NY // 2, NZ // 2), jnp.float32) ** shard_levels(splits[1], (27, LX, NY // 2, NZ // 2), ((1, 16), (2, 8), (3, 4)), -0.2, 0.2), 0.85, 1.15)
    fluid_mask = with_ends((jax.random.randint(splits[2], (NX, NY, NZ), 0, 8) < 7).astype(jnp.int32), jax.random.fold_in(splits[2], 1), 0, 1)
    inflow = jnp.clip(0.02 + 0.06 * jax.random.uniform(splits[3], (NY // 2, NZ // 2), jnp.float32) ** shard_levels(splits[3], (NY // 2, NZ // 2), ((0, 8), (1, 4)), -0.2, 0.2), 0.02, 0.08)
    part_dest_keys = jax.random.split(jax.random.fold_in(splits[4], 1), N_GX * N_GY * N_GZ * P_DEV // P_DEV)
    part_dest_turns = jax.random.permutation(jax.random.fold_in(splits[4], 3), N_GX * N_GY * N_GZ * P_DEV // P_DEV)
    part_dest = jax.vmap(lambda own, number: routed_block(jax.random.fold_in(splits[4], 2), own, number, P_DEV, N_GX, 1, CAP, 2))(part_dest_keys, part_dest_turns).reshape((N_GX, N_GY, N_GZ, P_DEV, 1))
    part_cell = draw_part_cell(jax.random.fold_in(splits[9], 71), 0)
    part_vel = noise(splits[6], (N_GX, N_GY, N_GZ, 3, P_DEV), 0.05, 0.3, ((0, 16), (1, 8), (2, 4)), jnp.float32)
    part_frac = jnp.clip(1.0 * jax.random.uniform(splits[7], (N_GX, N_GY, N_GZ, 3, P_DEV), jnp.float32) ** shard_levels(splits[7], (N_GX, N_GY, N_GZ, 3, P_DEV), ((0, 16), (1, 8), (2, 4)), -0.2, 0.2), 0.0, 1.0)
    part_drag = jnp.clip(jnp.exp(math.log(0.5) - 2.3025851 * jax.random.uniform(splits[8], (N_GX, N_GY, N_GZ, P_DEV), jnp.float32) ** shard_levels(splits[8], (N_GX, N_GY, N_GZ, P_DEV), ((0, 16), (1, 8), (2, 4)), -0.2, 0.2)), 0.05, 0.5)
    return {"populations": populations, "coarse_populations": coarse_populations, "fluid_mask": fluid_mask, "inflow": inflow, "part_dest": part_dest, "part_cell": part_cell, "part_vel": part_vel, "part_frac": part_frac, "part_drag": part_drag}


tau_fine = 1.3
tau_coarse = 0.9
stencil_ints = [(along_x, along_y, along_z) for along_x in (-1, 0, 1) for along_y in (-1, 0, 1) for along_z in (-1, 0, 1)]
stencil = np.array(stencil_ints, np.float32)
lattice_weights = np.array([8.0 / 27.0, 2.0 / 27.0, 1.0 / 54.0, 1.0 / 216.0], np.float32)[np.abs(stencil).sum(1).astype(np.int32)]
prolong_factor = (tau_fine - 1.0) / (2.0 * tau_coarse)
restrict_factor = 2.0 * (tau_coarse - 1.0) / tau_fine


def moments(normal):
    shape_tail = (1,) * (normal.ndim - 1)
    scaled = normal * lattice_weights.reshape((27,) + shape_tail)
    density = jnp.sum(scaled, axis=0)
    momentum = jnp.tensordot(stencil.T, scaled, axes=1, precision=lax.Precision.HIGHEST)
    return density, momentum


def equilibrium(density, velocity):
    projected = jnp.tensordot(stencil, velocity, axes=1, precision=lax.Precision.HIGHEST)
    square = jnp.sum(velocity * velocity, axis=0)
    return density * (1.0 + 3.0 * projected + 4.5 * projected * projected - 1.5 * square)


def collide(normal, fluid_ones, body_force, tau_value):
    density, momentum = moments(normal)
    safe_density = density + (1.0 - fluid_ones)
    velocity = momentum / safe_density + tau_value * body_force / safe_density
    return fluid_ones * (normal - (normal - equilibrium(safe_density, velocity)) / tau_value)


def interface(normal, factor):
    density, momentum = moments(normal)
    settled = equilibrium(density, momentum / density)
    return settled + factor * (normal - settled)


def restrict(normal):
    surface = normal[:, 0:2]
    half_y = surface.shape[2] // 2
    half_z = surface.shape[3] // 2
    summed = surface.reshape(27, 2, half_y, 2, half_z, 2).sum(axis=(1, 3, 5))
    return interface(0.125 * summed, restrict_factor)


def refine_layer(boundary):
    return jnp.repeat(jnp.repeat(boundary, 2, axis=1), 2, axis=2)


def stream(padded, collided, fluid_ones):
    extent = collided.shape[1:]
    result = []
    for number in range(27):
        shift_x, shift_y, shift_z = stencil_ints[number]
        anchor_x = 1 - shift_x
        anchor_y = 1 - shift_y
        anchor_z = 1 - shift_z
        source = padded[number, anchor_x:anchor_x + extent[0], anchor_y:anchor_y + extent[1], anchor_z:anchor_z + extent[2]]
        open_flag = padded[27, anchor_x:anchor_x + extent[0], anchor_y:anchor_y + extent[1], anchor_z:anchor_z + extent[2]]
        result.append(open_flag * source + (1.0 - open_flag) * collided[26 - number])
    return fluid_ones * jnp.stack(result)


def with_flag(boundary):
    return jnp.concatenate([boundary, jnp.ones((1,) + boundary.shape[1:], boundary.dtype)], 0)


def build_padded(collided, flags, left_layer, right_layer):
    stacked = jnp.concatenate([collided, flags[None]], 0)
    padded = jnp.pad(stacked, ((0, 0), (1, 1), (1, 1), (1, 1)))
    padded = padded.at[:, 0, 1:-1, 1:-1].set(with_flag(left_layer))
    if right_layer is None:
        padded = padded.at[:, -1].set(padded[:, -2])
    else:
        padded = padded.at[:, -1, 1:-1, 1:-1].set(with_flag(right_layer))
    return padded


def deposit(velocity_flat, cell_base, part_velocity, drag_values, fraction, stride_x, stride_y):
    corners = []
    sampled = jnp.zeros_like(part_velocity)
    for corner in range(8):
        offset_x = corner // 4
        offset_y = (corner // 2) % 2
        offset_z = corner % 2
        weight = (fraction[0] if offset_x else 1.0 - fraction[0]) * (fraction[1] if offset_y else 1.0 - fraction[1]) * (fraction[2] if offset_z else 1.0 - fraction[2])
        corner_index = cell_base + offset_x * stride_x + offset_y * stride_y + offset_z
        sampled = sampled + weight * velocity_flat[:, corner_index]
        corners.append((weight, corner_index))
    impulse = drag_values * (part_velocity - sampled)
    body_force = jnp.zeros_like(velocity_flat)
    for weight, corner_index in corners:
        body_force = body_force.at[:, corner_index].add(weight * impulse)
    return body_force


def reference(populations, coarse_populations, fluid_mask, inflow, part_dest, part_cell, part_vel, part_frac, part_drag):
    open_cells = fluid_mask.astype(jnp.float32)
    density, momentum = moments(populations)
    safe_density = density + (1.0 - open_cells)
    velocity_flat = (momentum / safe_density).reshape(3, -1)
    slab_ids = part_dest[..., 0]
    column_ids = jnp.arange(N_GY, dtype=jnp.int32)[None, :, None, None]
    row_ids = jnp.arange(N_GZ, dtype=jnp.int32)[None, None, :, None]
    local_x = part_cell // (CY * CZ)
    local_y = (part_cell // CZ) % CY
    local_z = part_cell % CZ
    global_cell = ((slab_ids * CX + local_x) * NY + column_ids * CY + local_y) * NZ + row_ids * CZ + local_z
    body_force = deposit(velocity_flat, global_cell.reshape(-1), jnp.moveaxis(part_vel, 3, 0).reshape(3, -1), part_drag.reshape(-1), jnp.moveaxis(part_frac, 3, 0).reshape(3, -1), NY * NZ, NZ)
    body_force = body_force.reshape((3,) + open_cells.shape)
    restricted = restrict(populations)
    zeros_plane = jnp.zeros_like(inflow)
    inlet = equilibrium(1.0, jnp.stack([inflow, zeros_plane, zeros_plane]))
    coarse_collided = collide(coarse_populations, 1.0, 0.0, tau_coarse)
    coarse_flags = jnp.ones(coarse_populations.shape[1:], jnp.float32)
    coarse_next = stream(build_padded(coarse_collided, coarse_flags, inlet, restricted), coarse_collided, 1.0)
    start_ghost = refine_layer(interface(coarse_populations[:, -1], prolong_factor))
    collided = collide(populations, open_cells, body_force, tau_fine)
    middle = stream(build_padded(collided, open_cells, start_ghost, None), collided, open_cells)
    late_ghost = refine_layer(interface(0.5 * (coarse_populations[:, -1] + coarse_next[:, -1]), prolong_factor))
    collided = collide(middle, open_cells, body_force, tau_fine)
    finished = stream(build_padded(collided, open_cells, late_ghost, None), collided, open_cells)
    return finished, coarse_next
```

```python
import jax
import jax.numpy as jnp
from jax import lax
from jax.experimental import pallas as pl
from jax.experimental.pallas import tpu as pltpu
from jax.sharding import Mesh, PartitionSpec as P

tau_fine = 1.3
tau_coarse = 0.9
prolong_factor = (tau_fine - 1.0) / (2.0 * tau_coarse)
restrict_factor = 2.0 * (tau_coarse - 1.0) / tau_fine
stencil = [(a, b, c) for a in (-1, 0, 1) for b in (-1, 0, 1) for c in (-1, 0, 1)]
class_weight = (8.0 / 27.0, 2.0 / 27.0, 1.0 / 54.0, 1.0 / 216.0)
wall = -1e30
limit = -1e29


def moving(axis, way):
    return [i for i in range(27) if stencil[i][axis] == way]


UP = [moving(axis, 1) for axis in range(3)]
DOWN = [moving(axis, -1) for axis in range(3)]

T_VEL, T_COARSE, T_GHOST, T_FACE = 28, 31, 36, 50
X_COARSE, T_X = 80, 89

z_items = [(0, x, ch) for x in range(1, 7) for ch in range(31)]
z_items += [(0, 0, i) for i in UP[0]] + [(0, 7, i) for i in DOWN[0]]
z_deep = [(1, x, j) for x in range(1, 7) for j in range(9)]


def z_layout(way):
    inward = UP[2] if way > 0 else DOWN[2]
    items = list(z_items) + [(1, x, inward[j]) for (_, x, j) in z_deep]
    items += [(1, 0, i) for i in inward if stencil[i][0] == 1]
    items += [(1, 7, i) for i in inward if stencil[i][0] == -1]
    return {item: spot for spot, item in enumerate(items)}


def c_layout(way):
    inward = UP[2] if way > 0 else DOWN[2]
    items = [("c", x, i) for x in range(1, 9) for i in inward]
    items += [("c", 0, i) for i in inward if stencil[i][0] == 1]
    items += [("c", 9, i) for i in inward if stencil[i][0] == -1]
    items += [("g", which, i, d) for which in range(3) for i in range(27) for d in range(2)]
    items += [("i",)]
    return {item: spot for spot, item in enumerate(items)}


ZL = {1: z_layout(1), -1: z_layout(-1)}
CL = {1: c_layout(1), -1: c_layout(-1)}


def roll(value, by, axis):
    by = by % value.shape[axis]
    return value if by == 0 else pltpu.roll(value, by, axis)


def iota(shape, axis):
    return lax.broadcasted_iota(jnp.int32, shape, axis)


def dot(a, b, contract=(1, 0)):
    return lax.dot_general(
        a,
        b,
        (((contract[0],), (contract[1],)), ((), ())),
        precision=lax.Precision.HIGHEST,
        preferred_element_type=jnp.float32,
    )


def moments(n):
    totals = [n[13], None, None, None]
    parts = [[None] * 4 for _ in range(3)]
    for i in range(14, 27):
        c = stencil[i]
        k = abs(c[0]) + abs(c[1]) + abs(c[2])
        both, odd = n[i] + n[26 - i], n[i] - n[26 - i]
        totals[k] = both if totals[k] is None else totals[k] + both
        for axis in range(3):
            if c[axis]:
                have = parts[axis][k]
                if have is None:
                    parts[axis][k] = odd if c[axis] > 0 else -odd
                else:
                    parts[axis][k] = have + odd if c[axis] > 0 else have - odd
    density = sum(class_weight[k] * totals[k] for k in range(4))
    momentum = [sum(class_weight[k] * parts[axis][k] for k in (1, 2, 3)) for axis in range(3)]
    return density, momentum


def equilibrium(s, u):
    base = s - (1.5 * (u[0] * u[0] + u[1] * u[1] + u[2] * u[2])) * s
    s3, s45 = 3.0 * s, 4.5 * s
    out = [None] * 27
    out[13] = base
    for i in range(14, 27):
        cu = None
        for axis in range(3):
            c = stencil[i][axis]
            if c:
                if cu is None:
                    cu = u[axis] if c > 0 else -u[axis]
                else:
                    cu = cu + u[axis] if c > 0 else cu - u[axis]
        even, odd = base + s45 * (cu * cu), s3 * cu
        out[i], out[26 - i] = even + odd, even - odd
    return out


def collide(n, g, force, tau):
    density, m = moments(n)
    s = jnp.where(density == 0.0, 1.0, density) if g is None else density + (1.0 - g)
    inverse = 1.0 / s
    if force is not None:
        m = [m[k] + tau * force[k] for k in range(3)]
    e = equilibrium(s * (1.0 / tau), [v * inverse for v in m])
    post = [(1.0 - 1.0 / tau) * n[i] + e[i] for i in range(27)]
    return post if g is None else [jnp.where(g > 0.0, p, wall) for p in post]


def interface(n, factor):
    density, m = moments(n)
    density = jnp.where(density == 0.0, 1.0, density)
    inverse = 1.0 / density
    e = equilibrium(density, [v * inverse for v in m])
    return [e[i] + factor * (n[i] - e[i]) for i in range(27)]


S_H, S_CORE, S_ODD, S_FIRST, S_LAST, S_YLO, S_YHI, S_ZLO, S_ZHI = range(9)


def pack_kernel(sc, pop, cpop, mask, inflow, pdest, pcell, pvel, pfrac, pdrag, ymsg, outbox, vel, cc, rc, rs):
    h = sc[S_H]
    dest = pdest[...]
    onehot = (iota((16, 256), 0) == dest).astype(jnp.float32)
    earlier = (iota((256, 256), 0) < iota((256, 256), 1)).astype(jnp.bfloat16)
    before = jnp.dot(onehot.astype(jnp.bfloat16), earlier, preferred_element_type=jnp.float32)
    rank = jnp.sum(onehot * before, axis=0, keepdims=True).astype(jnp.int32)
    slot = (iota((32, 256), 0) == rank).astype(jnp.float32)
    row = iota((64, 256), 0)
    hit = (row >> 2) == dest
    odd = (row & 1) == 1
    fields = [pvel[k : k + 1, :] for k in range(3)] + [pdrag[...]]
    fields += [pfrac[k : k + 1, :] for k in range(3)] + [pcell[...].astype(jnp.float32)]
    for q in range(4):
        values = jnp.where(hit, jnp.where(odd, fields[4 + q], fields[q]), 0.0)
        outbox[:, 32 * q : 32 * q + 32] = dot(values, slot, (1, 1))
    for x in range(4):
        density, m = moments([pop[i, x] for i in range(27)])
        inverse = 1.0 / (density + (1.0 - mask[x].astype(jnp.float32)))
        for k in range(3):
            vel[k, x] = m[k] * inverse
    rc[...] = jnp.zeros(rc.shape, jnp.float32)
    for i in range(27):
        rc[i, :, 0:4, 0:64] = cpop[i]
    for x in range(8):
        post = collide([rc[i, x] for i in range(27)], None, None, tau_coarse)
        for i in range(27):
            cc[x, i] = post[i]
    pair = jnp.concatenate([pop[i, 0] + pop[i, 1] for i in range(27)], axis=0)
    narrow = ((iota((128, 128), 0) >> 1) == iota((128, 128), 1)).astype(jnp.float32)
    down, across = iota((216, 216), 0), iota((216, 216), 1)
    low = ((down >> 3) == (across >> 3)) & (((across & 7) >> 1) == (down & 7))
    mean = 0.125 * dot(low.astype(jnp.float32), dot(pair, narrow))
    settled = interface([mean[8 * i : 8 * i + 8] for i in range(27)], restrict_factor)
    for i in range(27):
        rs[i] = settled[i]
    for top in (1, 0):
        face = h if top else 1 - h
        near, third, crow, grow = (6, 5, 3, 2) if top else (0, 2, 0, 0)
        for x in range(4):
            for t in range(27):
                ymsg[face, t, 2 * x : 2 * x + 2, :] = pop[t, x, near : near + 2, :]
            ymsg[face, 27, 2 * x : 2 * x + 2, :] = mask[x, near : near + 2, :].astype(jnp.float32)
        for k in range(3):
            ymsg[face, T_VEL + k] = jnp.zeros((8, 128), jnp.float32)
            for x in range(4):
                ymsg[face, T_VEL + k, x : x + 1, :] = vel[k, x, third : third + 1, :]
        for j, i in enumerate(UP[1] if top else DOWN[1]):
            lane = 64 * (j // 5)
            for x in range(8):
                ymsg[face, T_COARSE + j % 5, x : x + 1, lane : lane + 64] = cc[x, i, crow : crow + 1, 0:64]
        ymsg[face, T_COARSE + 4, :, 64:128] = jnp.zeros((8, 64), jnp.float32)
        for t in range(14):
            ymsg[face, T_GHOST + t] = jnp.zeros((8, 128), jnp.float32)
        for t in range(27):
            lane = 64 * (t // 14)
            tile = T_GHOST + t % 14
            ymsg[face, tile, 0:2, lane : lane + 64] = rc[t, 6, grow : grow + 2, 0:64]
            ymsg[face, tile, 2:4, lane : lane + 64] = rc[t, 7, grow : grow + 2, 0:64]
            ymsg[face, tile, 4:6, lane : lane + 64] = rs[t, grow : grow + 2, 0:64]
        ymsg[face, T_GHOST + 13, 0:1, 64:128] = inflow[crow : crow + 1, :]


def particle_fields(rows):
    lane = iota((2, 128), 1) >> 5
    chunks = [[] for _ in range(4)]
    for k in range(4):
        turned = [[roll(rows[4 * k + j], 32 * s, 1) for s in range(4)] for j in range(4)]
        for q in range(4):
            value = turned[0][(0 - q) % 4]
            for j in range(1, 4):
                value = jnp.where(lane == j, turned[j][(j - q) % 4], value)
            chunks[q].append(value)
    flat = [jnp.concatenate(chunks[q], axis=1) for q in range(4)]
    return [flat[f % 4][f // 4 : f // 4 + 1, :] for f in range(8)]


def deposit(fields, velocity, xr, yr, keep):
    rows = velocity[0].shape[0]
    count = fields[0].shape[1]
    cell = fields[7].astype(jnp.int32)
    ix, iy, iz = cell >> 10, (cell >> 7) & 7, cell & 127
    fx, fy, fz = fields[4:7]
    lane = iota((128, count), 0)
    along = jnp.where(lane == iz, 1.0 - fz, jnp.where(lane == iz + 1, fz, 0.0))
    across = jnp.where(xr == ix, 1.0 - fx, jnp.where(xr == ix + 1, fx, 0.0))
    across = across * jnp.where(yr == iy, 1.0 - fy, jnp.where(yr == iy + 1, fy, 0.0))
    seen = dot(jnp.concatenate(velocity, axis=0), along)
    pushes = []
    for k in range(3):
        sampled = jnp.sum(seen[k * rows : (k + 1) * rows] * across, axis=0, keepdims=True)
        impulse = fields[3] * (fields[k] - sampled)
        pushes.append(impulse * across[0:keep])
    force = dot(jnp.concatenate(pushes, axis=0), along, (1, 1))
    return [force[k * keep : (k + 1) * keep] for k in range(3)]


def deposit_kernel(
    sc, pop, mask, vel, cc, rc, rs, inflow, near, fwd, arr, ye, xa, xb, ccy, sw, inf, hi, lo
):
    h = sc[S_H]
    lower = h == 0
    for t in range(T_FACE):
        hi[t] = jnp.where(lower, near[0, t], fwd[t])
        lo[t] = jnp.where(lower, fwd[t], near[0, t])
    own = particle_fields([arr[2 * s + h] for s in range(16)])
    partner = particle_fields([arr[2 * s + 1 - h] for s in range(16)])
    rows = []
    for s in range(16):
        tile = T_FACE + s // 2
        first, second = fwd[tile, 4 * (s % 2) : 4 * (s % 2) + 2, :], fwd[tile, 4 * (s % 2) + 2 : 4 * (s % 2) + 4, :]
        rows.append(jnp.where(lower, second, first))
    third = particle_fields(rows)
    high = [jnp.where(lower, a, b) for a, b in zip(partner, third)]
    low = [jnp.where(lower, b, a) for a, b in zip(partner, third)]
    rows32 = iota((32, 1), 0)
    force = deposit(
        own,
        [jnp.concatenate([vel[k, x] for x in range(4)], axis=0) for k in range(3)],
        rows32 >> 3,
        rows32 & 7,
        32,
    )
    rows16 = iota((16, 1), 0)
    x16 = jnp.where(rows16 < 8, rows16 >> 1, rows16 - 8)
    sides = []
    for face, fields, base, last in ((hi, high, 0, 2), (lo, low, 6, 5)):
        n = [face[i] for i in range(27)]
        g = face[27]
        density, m = moments(n)
        inverse = 1.0 / (density + (1.0 - g))
        velocity = [jnp.concatenate([m[k] * inverse, face[T_VEL + k]], axis=0) for k in range(3)]
        y16 = jnp.where(rows16 < 8, base + (rows16 & 1), last)
        f = deposit(fields, velocity, x16, y16, 8)
        sides.append(collide(n, g, f, tau_fine) + [g] + f)
    row = iota((8, 128), 0)
    for x in range(4):
        g = mask[x].astype(jnp.float32)
        f = [force[k][8 * x : 8 * x + 8] for k in range(3)]
        mine = collide([pop[i, x] for i in range(27)], g, f, tau_fine) + [g] + f
        for ch in range(31):
            ye[x, ch, 0:8, :] = mine[ch]
            ye[x, ch, 8:16, :] = jnp.where(
                row < 2,
                roll(sides[0][ch], -2 * x, 0),
                jnp.where(row >= 6, roll(sides[1][ch], 6 - 2 * x, 0), 0.0),
            )
    ccy[...] = cc[...]
    has_hi, has_lo = sc[S_YHI] == 1, sc[S_YLO] == 1
    for face, way, has, r in ((hi, DOWN[1], has_hi, 4), (lo, UP[1], has_lo, 7)):
        for j, i in enumerate(way):
            lane = 64 * (j // 5)
            for x in range(8):
                value = face[T_COARSE + j % 5, x : x + 1, lane : lane + 64]
                ccy[x, i, r : r + 1, 0:64] = jnp.where(has, value, wall)
    even = sc[S_CORE] == 0
    for ch in range(40):
        up = ye[3, ch] if ch < 31 else ye[2, UP[0][ch - 31]]
        down = ye[0, ch] if ch < 31 else ye[1, DOWN[0][ch - 31]]
        a, b = jnp.where(even, up, down), jnp.where(even, down, up)
        xa[2 * ch], xa[2 * ch + 1] = a[0:8], a[8:16]
        xb[2 * ch], xb[2 * ch + 1] = b[0:8], b[8:16]
    for j in range(9):
        up, down = ccy[7, UP[0][j]], ccy[0, DOWN[0][j]]
        xa[X_COARSE + j] = jnp.where(even, up, down)
        xb[X_COARSE + j] = jnp.where(even, down, up)
    sw[...] = jnp.zeros(sw.shape, jnp.float32)
    inf[...] = jnp.zeros((8, 128), jnp.float32)
    inf[0:4, 0:64] = inflow[...]
    inf[4:5, 0:64] = hi[T_GHOST + 13, 0:1, 64:128]
    inf[7:8, 0:64] = lo[T_GHOST + 13, 0:1, 64:128]

    @pl.when(sc[S_FIRST] == 1)
    def _():
        for t in range(27):
            lane, tile = 64 * (t // 14), T_GHOST + t % 14
            sw[t, 0:4, 0:64] = rs[t, 0:4, 0:64]
            sw[t, 4:6, 0:64] = hi[tile, 4:6, lane : lane + 64]
            sw[t, 6:8, 0:64] = lo[tile, 4:6, lane : lane + 64]

    @pl.when(sc[S_FIRST] == 0)
    def _():
        for t in range(27):
            lane, tile = 64 * (t // 14), T_GHOST + t % 14
            for part in range(2):
                to = 64 * part
                sw[t, 0:4, to : to + 64] = rc[t, 6 + part, 0:4, 0:64]
                sw[t, 4:6, to : to + 64] = hi[tile, 2 * part : 2 * part + 2, lane : lane + 64]
                sw[t, 6:8, to : to + 64] = lo[tile, 2 * part : 2 * part + 2, lane : lane + 64]


def x_tile(ye, up, down, x, ch):
    if 2 <= x <= 5:
        return ye[x - 2, ch]
    face = down if x < 2 else up
    slot = ch if x in (1, 6) else 31 + (UP[0] if x == 0 else DOWN[0]).index(ch)
    return jnp.concatenate([face(2 * slot), face(2 * slot + 1)], axis=0)


def pick(sc, index, a, b):
    even = sc[index] == 0
    return (lambda t: jnp.where(even, a[t], b[t])), (lambda t: jnp.where(even, b[t], a[t]))


def column_kernel(sc, ye, xar, xbr, swr, ccy, sw, inf, za, zb):
    up, down = pick(sc, S_CORE, xar, xbr)
    lane = iota((16, 128), 1)
    lane8 = iota((8, 128), 1)
    made = {}
    for way in (1, -1):
        tiles = [jnp.zeros((16, 128), jnp.float32) for _ in range(3)]
        for (depth, x, ch), spot in ZL[way].items():
            source = 127 - depth if way > 0 else depth
            value = roll(x_tile(ye, up, down, x, ch), spot - source, 1)
            tiles[spot // 128] = jnp.where(lane == spot % 128, value, tiles[spot // 128])
        out = [t[8 * k : 8 * k + 8] for t in tiles for k in range(2)]
        tiles = [jnp.zeros((8, 128), jnp.float32) for _ in range(2)]
        for item, spot in CL[way].items():
            if item[0] == "c":
                _, x, i = item
                if x == 0:
                    value = down(X_COARSE + UP[0].index(i))
                elif x == 9:
                    value = up(X_COARSE + DOWN[0].index(i))
                else:
                    value = ccy[x - 1, i]
                source = 63 if way > 0 else 0
            elif item[0] == "g":
                _, which, i, depth = item
                value = sw[i] if which == 2 else swr[i]
                source = (63 - depth if way > 0 else depth) + (64 if which == 1 else 0)
            else:
                value = inf[...]
                source = 63 if way > 0 else 0
            value = roll(value, spot - source, 1)
            tiles[spot // 128] = jnp.where(lane8 == spot % 128, value, tiles[spot // 128])
        made[way] = out + tiles
    even = sc[S_ODD] == 0
    for t in range(8):
        za[t] = jnp.where(even, made[1][t], made[-1][t])
        zb[t] = jnp.where(even, made[-1][t], made[1][t])


def step_kernel(
    sc, ye, xar, xbr, swr, ccy, sw, inf, zar, zbr, fine, coarse, p1, p2, gx, fx, ce, gr, late
):
    up, down = pick(sc, S_CORE, xar, xbr)
    zup, zdown = pick(sc, S_ODD, zar, zbr)
    has_yhi, has_ylo, has_zhi, has_zlo = [sc[k] == 1 for k in (S_YHI, S_YLO, S_ZHI, S_ZLO)]
    first, last = sc[S_FIRST] == 1, sc[S_LAST] == 1
    fz_up = [jnp.concatenate([zup(2 * k), zup(2 * k + 1)], axis=0) for k in range(3)]
    fz_down = [jnp.concatenate([zdown(2 * k), zdown(2 * k + 1)], axis=0) for k in range(3)]
    cz_up, cz_down = [zup(6), zup(7)], [zdown(6), zdown(7)]
    lane = iota((16, 128), 1)
    lane8 = iota((8, 128), 1)

    def side(x, ch):
        blank = wall if ch < 27 else 0.0
        value = jnp.zeros((16, 128), jnp.float32)
        for depth in range(2):
            for way, source, has, at in ((-1, fz_up, has_zhi, depth), (1, fz_down, has_zlo, 127 - depth)):
                spot = ZL[way].get((depth, x, ch))
                if spot is not None:
                    moved = jnp.where(has, roll(source[spot // 128], at - spot, 1), blank)
                    value = jnp.where(lane == at, moved, value)
        return value

    for x in range(8):
        for ch in range(31) if 0 < x < 7 else (UP[0] if x == 0 else DOWN[0]):
            main, rest = x_tile(ye, up, down, x, ch), side(x, ch)
            if ch < 27:
                to = p1.at[x, ch]
            elif ch == 27:
                to = gx.at[x - 1]
            else:
                to = fx.at[x - 1, ch - 28]
            to[:, 0:128] = main
            to[:, 128:256] = rest

    row8 = iota((8, 128), 0)
    inside = (row8 < 4) | ((row8 < 6) & has_yhi) | ((row8 >= 6) & has_ylo)
    inside = inside & (
        (lane8 < 64) | ((lane8 >= 64) & (lane8 < 66) & has_zhi) | ((lane8 >= 126) & has_zlo)
    )

    def c_side(value, up_item, down_item, blank, at=64, end=127):
        for way, source, has, item, to in ((-1, cz_up, has_zhi, up_item, at), (1, cz_down, has_zlo, down_item, end)):
            spot = CL[way].get(item)
            if spot is not None:
                moved = jnp.where(has, roll(source[spot // 128], to - spot, 1), blank)
                value = jnp.where(lane8 == to, moved, value)
        return value

    def ghost(which, i):
        value = sw[i] if which == 2 else swr[i]
        if which == 1:
            value = roll(value, 64, 1)
        value = jnp.where(lane8 < 64, value, 0.0)
        for depth in range(2):
            item = ("g", which, i, depth)
            value = c_side(value, item, item, 0.0, 64 + depth, 127 - depth)
        return value

    for x in range(8):
        for i in range(27):
            ce[x + 1, i] = c_side(ccy[x, i], ("c", x + 1, i), ("c", x + 1, i), wall)
    inflow = c_side(inf[...], ("i",), ("i",), 0.0)
    zero = jnp.zeros((8, 128), jnp.float32)
    inlet = equilibrium(jnp.ones((8, 128), jnp.float32), [inflow, zero, zero])
    for j in range(9):
        i = UP[0][j]
        came = c_side(down(X_COARSE + j), ("c", 0, i), ("c", 0, i), wall)
        ce[0, i] = jnp.where(first, jnp.where(inside, inlet[i], wall), came)
        i = DOWN[0][j]
        came = c_side(up(X_COARSE + j), ("c", 9, i), ("c", 9, i), wall)
        ce[9, i] = jnp.where(last, jnp.where(inside, ghost(0, i), wall), came)
    for i in range(27):
        a, b, c = stencil[i]
        for x in range(8):
            value = roll(roll(ce[x + 1 - a, i], b, 0), c, 1)
            value = jnp.where(value > limit, value, ce[x + 1, 26 - i])
            coarse[i, x] = value[0:4, 0:64]

    @pl.when(first)
    def _():
        n126 = [ghost(0, i) for i in range(27)]
        post = collide(n126, None, None, tau_coarse)
        for i in range(27):
            gr[0, i] = jnp.where(inside, post[i], wall)
        n127 = [ghost(1, i) for i in range(27)]
        post = collide(n127, None, None, tau_coarse)
        for i in range(27):
            gr[1, i] = jnp.where(inside, post[i], wall)
            gr[2, i] = jnp.where(inside, ghost(2, i), wall)
        later = []
        for i in range(27):
            a, b, c = stencil[i]
            value = roll(roll(gr[1 - a, i], b, 0), c, 1)
            value = jnp.where(value > limit, value, gr[1, 26 - i])
            later.append(jnp.where(inside, 0.5 * (n127[i] + value), 0.0))
        wide = ((iota((128, 256), 1) >> 1) == iota((128, 256), 0)).astype(jnp.float32)
        tall = ((iota((432, 216), 0) >> 1) == iota((432, 216), 1)).astype(jnp.float32)
        row16, lane256 = iota((16, 256), 0), iota((16, 256), 1)
        within = (row16 < 8) | ((row16 < 12) & has_yhi) | ((row16 >= 12) & has_ylo)
        within = within & (
            (lane256 < 128) | ((lane256 < 132) & has_zhi) | ((lane256 >= 252) & has_zlo)
        )
        for layer, to in ((n127, p1.at[1]), (later, late)):
            layer = interface(layer, prolong_factor)
            fines = dot(tall, dot(jnp.concatenate(layer, axis=0), wide))
            for i in range(27):
                to[i] = jnp.where(within, fines[16 * i : 16 * i + 16], wall)

    @pl.when(last)
    def _():
        for i in range(27):
            p1[6, i] = p1[5, i]

    def stream_layer(m, carry):
        g = gx[m]
        for i in range(27):
            a, b, c = stencil[i]
            value = roll(roll(p1[m + 1 - a, i], b, 0), c, 1)
            value = jnp.where(value > limit, value, p1[m + 1, 26 - i])
            p2[m, i] = jnp.where(g > 0.0, value, 0.0)
        return carry

    lax.fori_loop(0, 6, stream_layer, 0)

    def collide_layer(m, carry):
        for y in range(2):
            for z in range(2):
                rows, lanes = slice(8 * y, 8 * y + 8), slice(128 * z, 128 * z + 128)
                post = collide(
                    [p2[m, i, rows, lanes] for i in range(27)],
                    gx[m, rows, lanes],
                    [fx[m, k, rows, lanes] for k in range(3)],
                    tau_fine,
                )
                for i in range(27):
                    p2[m, i, rows, lanes] = post[i]
        return carry

    lax.fori_loop(0, 6, collide_layer, 0)

    @pl.when(first)
    def _():
        for i in range(27):
            p2[0, i] = late[i]

    @pl.when(last)
    def _():
        for i in range(27):
            p2[5, i] = p2[4, i]

    def finish_layer(x, carry):
        g = gx[x + 1, 0:8, 0:128]
        for i in range(27):
            a, b, c = stencil[i]
            value = roll(roll(p2[x + 1 - a, i], b, 0), c, 1)[0:8, 0:128]
            value = jnp.where(value > limit, value, p2[x + 1, 26 - i, 0:8, 0:128])
            fine[i, x] = jnp.where(g > 0.0, value, 0.0)
        return carry

    lax.fori_loop(0, 4, finish_layer, 0)


def f32(*shape):
    return jax.ShapeDtypeStruct(shape, jnp.float32)


def call(kernel, name, out_shape, scratch, *args):
    vmem = pl.BlockSpec(memory_space=pltpu.VMEM)
    return pl.pallas_call(
        kernel,
        out_shape=out_shape,
        in_specs=[pl.BlockSpec(memory_space=pltpu.SMEM)] + [vmem] * (len(args) - 1),
        out_specs=[vmem] * len(out_shape),
        scratch_shapes=[pltpu.VMEM(s, jnp.float32) for s in scratch],
        compiler_params=pltpu.CompilerParams(vmem_limit_bytes=40 * 1024 * 1024),
        name=name,
    )(*args)


def body(pop, cpop, mask, inflow, part_dest, part_cell, part_vel, part_frac, part_drag):
    gx, gy, h, gz = [lax.axis_index(a) for a in ("gx", "y", "h", "gz")]
    n_gx, n_y, n_gz = lax.axis_size("gx"), lax.axis_size("y"), lax.axis_size("gz")
    row = gy * 2 + h
    sc = jnp.stack(
        [
            h,
            gx % 2,
            gz % 2,
            (gx == 0).astype(jnp.int32),
            (gx == n_gx - 1).astype(jnp.int32),
            (row > 0).astype(jnp.int32),
            (row < 2 * n_y - 1).astype(jnp.int32),
            (gz > 0).astype(jnp.int32),
            (gz < n_gz - 1).astype(jnp.int32),
        ]
    ).astype(jnp.int32)
    ymsg, outbox, vel, cc, rc, rs = call(
        pack_kernel,
        "pack",
        [
            f32(2, T_FACE, 8, 128),
            f32(64, 128),
            f32(3, 4, 8, 128),
            f32(8, 27, 8, 128),
            f32(27, 8, 8, 128),
            f32(27, 8, 128),
        ],
        [],
        sc,
        pop,
        cpop,
        mask,
        inflow,
        part_dest.reshape(1, 256),
        part_cell.reshape(1, 256),
        part_vel.reshape(3, 256),
        part_frac.reshape(3, 256),
        part_drag.reshape(1, 256),
    )
    near = lax.ppermute(ymsg, "h", [(0, 1), (1, 0)])
    arr = lax.all_to_all(outbox.reshape(2 * n_gx, 2, 128), ("gx", "h"), 0, 0, tiled=True)
    onward = [(2 * y, 2 * y + 2) for y in range(n_y - 1)]
    onward += [(2 * y + 3, 2 * y + 1) for y in range(n_y - 1)]
    fwd = lax.ppermute(jnp.concatenate([near[1], arr.reshape(8, 8, 128)], axis=0), ("y", "h"), onward)
    ye, xa, xb, ccy, sw, inf = call(
        deposit_kernel,
        "deposit",
        [
            f32(4, 31, 16, 128),
            f32(T_X, 8, 128),
            f32(T_X, 8, 128),
            f32(8, 27, 8, 128),
            f32(27, 8, 128),
            f32(8, 128),
        ],
        [(T_FACE, 8, 128), (T_FACE, 8, 128)],
        sc,
        pop,
        mask,
        vel,
        cc,
        rc,
        rs,
        inflow,
        near,
        fwd,
        arr,
    )
    swr = lax.ppermute(sw, "gx", [(0, n_gx - 1), (n_gx - 1, 0)])
    xar = lax.ppermute(xa, "gx", [(i, i ^ 1) for i in range(n_gx)])
    inner = [(i, i + 1) for i in range(1, n_gx - 1, 2)]
    xbr = lax.ppermute(xb, "gx", inner + [(j, i) for i, j in inner])
    za, zb = call(
        column_kernel,
        "columns",
        [f32(8, 8, 128), f32(8, 8, 128)],
        [],
        sc,
        ye,
        xar,
        xbr,
        swr,
        ccy,
        sw,
        inf,
    )
    zar = lax.ppermute(za, "gz", [(i, i ^ 1) for i in range(n_gz)])
    inner = [(i, i + 1) for i in range(1, n_gz - 1, 2)]
    zbr = lax.ppermute(zb, "gz", inner + [(j, i) for i, j in inner])
    fine, coarse = call(
        step_kernel,
        "steps",
        [f32(27, 4, 8, 128), f32(27, 8, 4, 64)],
        [
            (8, 27, 16, 256),
            (6, 27, 16, 256),
            (6, 16, 256),
            (6, 3, 16, 256),
            (10, 27, 8, 128),
            (3, 27, 8, 128),
            (27, 16, 256),
        ],
        sc,
        ye,
        xar,
        xbr,
        swr,
        ccy,
        sw,
        inf,
        zar,
        zbr,
    )
    return fine, coarse


def solution(mesh):
    n_gx, n_gy, n_gz = [mesh.shape[a] for a in ("gx", "gy", "gz")]
    split = Mesh(mesh.devices.reshape(n_gx, n_gy // 2, 2, n_gz), ("gx", "y", "h", "gz"))
    gy = ("y", "h")
    return jax.shard_map(
        body,
        mesh=split,
        in_specs=(
            P(None, "gx", gy, "gz"),
            P(None, "gx", gy, "gz"),
            P("gx", gy, "gz"),
            P(gy, "gz"),
            P("gx", gy, "gz", None, None),
            P("gx", gy, "gz", None),
            P("gx", gy, "gz", None, None),
            P("gx", gy, "gz", None, None),
            P("gx", gy, "gz", None),
        ),
        out_specs=(P(None, "gx", gy, "gz"), P(None, "gx", gy, "gz")),
        check_vma=False,
    )
```

```python
import jax
import jax.numpy as jnp
from jax import lax
from jax.experimental import pallas as pl
from jax.experimental.pallas import tpu as pltpu
from jax.sharding import Mesh, PartitionSpec as P

tau_fine = 1.3
tau_coarse = 0.9
prolong_factor = (tau_fine - 1.0) / (2.0 * tau_coarse)
restrict_factor = 2.0 * (tau_coarse - 1.0) / tau_fine
stencil = [(a, b, c) for a in (-1, 0, 1) for b in (-1, 0, 1) for c in (-1, 0, 1)]
class_weight = (8.0 / 27.0, 2.0 / 27.0, 1.0 / 54.0, 1.0 / 216.0)
wall = -1e30
limit = -1e29


def moving(axis, way):
    return [i for i in range(27) if stencil[i][axis] == way]


UP = [moving(axis, 1) for axis in range(3)]
DOWN = [moving(axis, -1) for axis in range(3)]

T_DEEP, T_COARSE, T_FACE = 14, 23, 32
X_ROWS, X_COARSE, T_X = 40, 60, 69


def level_rows(way):
    rows = [(ch, 0) for ch in range(46)] + [(ch, 1) for ch in range(27)]
    rows += [(27 + j, 1) for j in range(9) if stencil[UP[0][j]][1] == way]
    rows += [(36 + j, 1) for j in range(9) if stencil[DOWN[0][j]][1] == way]
    spots = [(22, r, 64 * half) for r in range(4, 8) for half in range(2)]
    spots += [(27, r, 64) for r in range(8)]
    spots += [(t, r, 64 * half) for t in range(28, 32) for r in range(8) for half in range(2)]
    return dict(zip(rows, spots))


LEVEL = {1: level_rows(1), -1: level_rows(-1)}
T_SW = 18

z_items = [(0, x, ch) for x in range(1, 7) for ch in range(31)]
z_items += [(0, 0, i) for i in UP[0]] + [(0, 7, i) for i in DOWN[0]]
z_deep = [(1, x, j) for x in range(1, 7) for j in range(9)]


def z_layout(way):
    inward = UP[2] if way > 0 else DOWN[2]
    items = list(z_items) + [(1, x, inward[j]) for (_, x, j) in z_deep]
    items += [(1, 0, i) for i in inward if stencil[i][0] == 1]
    items += [(1, 7, i) for i in inward if stencil[i][0] == -1]
    return {item: spot for spot, item in enumerate(items)}


def c_layout(way):
    inward = UP[2] if way > 0 else DOWN[2]
    items = [("c", x, i) for x in range(1, 9) for i in inward]
    items += [("c", 0, i) for i in inward if stencil[i][0] == 1]
    items += [("c", 9, i) for i in inward if stencil[i][0] == -1]
    items += [("g", ch, 0) for ch in range(45)] + [("g", ch, 1) for ch in range(27)]
    items += [("g", 27 + j, 1) for j in range(9) if stencil[UP[0][j]][2] == way]
    items += [("g", 36 + j, 1) for j in range(9) if stencil[DOWN[0][j]][2] == way]
    items += [("i",)]
    return {item: spot for spot, item in enumerate(items)}


ZL = {1: z_layout(1), -1: z_layout(-1)}
CL = {1: c_layout(1), -1: c_layout(-1)}


def roll(value, by, axis):
    by = by % value.shape[axis]
    return value if by == 0 else pltpu.roll(value, by, axis)


def iota(shape, axis):
    return lax.broadcasted_iota(jnp.int32, shape, axis)


def dot(a, b, contract=(1, 0)):
    return lax.dot_general(
        a,
        b,
        (((contract[0],), (contract[1],)), ((), ())),
        precision=lax.Precision.HIGHEST,
        preferred_element_type=jnp.float32,
    )


def moments(n):
    totals = [n[13], None, None, None]
    parts = [[None] * 4 for _ in range(3)]
    for i in range(14, 27):
        c = stencil[i]
        k = abs(c[0]) + abs(c[1]) + abs(c[2])
        both, odd = n[i] + n[26 - i], n[i] - n[26 - i]
        totals[k] = both if totals[k] is None else totals[k] + both
        for axis in range(3):
            if c[axis]:
                have = parts[axis][k]
                if have is None:
                    parts[axis][k] = odd if c[axis] > 0 else -odd
                else:
                    parts[axis][k] = have + odd if c[axis] > 0 else have - odd
    density = sum(class_weight[k] * totals[k] for k in range(4))
    momentum = [sum(class_weight[k] * parts[axis][k] for k in (1, 2, 3)) for axis in range(3)]
    return density, momentum


def equilibrium(s, u):
    base = s - (1.5 * (u[0] * u[0] + u[1] * u[1] + u[2] * u[2])) * s
    s3, s45 = 3.0 * s, 4.5 * s
    out = [None] * 27
    out[13] = base
    for i in range(14, 27):
        cu = None
        for axis in range(3):
            c = stencil[i][axis]
            if c:
                if cu is None:
                    cu = u[axis] if c > 0 else -u[axis]
                else:
                    cu = cu + u[axis] if c > 0 else cu - u[axis]
        even, odd = base + s45 * (cu * cu), s3 * cu
        out[i], out[26 - i] = even + odd, even - odd
    return out


def collide(n, g, force, tau):
    density, m = moments(n)
    s = jnp.where(density == 0.0, 1.0, density) if g is None else density + (1.0 - g)
    inverse = 1.0 / s
    if force is not None:
        m = [m[k] + tau * force[k] for k in range(3)]
    e = equilibrium(s * (1.0 / tau), [v * inverse for v in m])
    post = [(1.0 - 1.0 / tau) * n[i] + e[i] for i in range(27)]
    return post if g is None else [jnp.where(g > 0.0, p, wall) for p in post]


def interface(n, factor):
    density, m = moments(n)
    density = jnp.where(density == 0.0, 1.0, density)
    inverse = 1.0 / density
    e = equilibrium(density, [v * inverse for v in m])
    return [e[i] + factor * (n[i] - e[i]) for i in range(27)]


S_H, S_CORE, S_ODD, S_FIRST, S_LAST, S_YLO, S_YHI, S_ZLO, S_ZHI = range(9)


def route_kernel(sc, pdest, pcell, pvel, pfrac, pdrag, anchor, outbox):
    del sc, anchor
    dest = pdest[...]
    onehot = (iota((16, 256), 0) == dest).astype(jnp.float32)
    earlier = (iota((256, 256), 0) < iota((256, 256), 1)).astype(jnp.bfloat16)
    before = jnp.dot(onehot.astype(jnp.bfloat16), earlier, preferred_element_type=jnp.float32)
    rank = jnp.sum(onehot * before, axis=0, keepdims=True).astype(jnp.int32)
    slot = (iota((32, 256), 0) == rank).astype(jnp.float32)
    row = iota((64, 256), 0)
    hit = (row >> 2) == dest
    odd = (row & 1) == 1
    fields = [pvel[0, 0, 0, k : k + 1, :] for k in range(3)] + [pdrag[...]]
    fields += [pfrac[0, 0, 0, k : k + 1, :] for k in range(3)] + [pcell[...].astype(jnp.float32)]
    for q in range(4):
        values = jnp.where(hit, jnp.where(odd, fields[4 + q], fields[q]), 0.0)
        outbox[:, 32 * q : 32 * q + 32] = dot(values, slot, (1, 1))


def pack_kernel(
    sc, pop_in, cpop_in, mask, inflow,
    far, near, vel, cc, r127, rs, pop, cpop, rc, mom, faces, sems,
):
    h = sc[S_H]
    copies = [pltpu.make_async_copy(pop_in, pop, sems.at[0]), pltpu.make_async_copy(cpop_in, cpop, sems.at[1])]
    for c in copies:
        c.start()
    rc[...] = jnp.zeros(rc.shape, jnp.float32)
    faces[...] = jnp.zeros(faces.shape, jnp.float32)
    for c in copies:
        c.wait()
    for x in range(4):
        density, m = moments([pop[i, x] for i in range(27)])
        inverse = 1.0 / (density + (1.0 - mask[x].astype(jnp.float32)))
        mom[0, x] = density
        for k in range(3):
            mom[k + 1, x] = m[k]
            vel[k, x] = m[k] * inverse
    for i in range(27):
        rc[i, :, 0:4, 0:64] = cpop[i]
        r127[i] = rc[i, 7]
    for x in range(8):
        post = collide([rc[i, x] for i in range(27)], None, None, tau_coarse)
        for i in range(27):
            cc[x, i] = post[i]
    pair = jnp.concatenate([pop[i, 0] + pop[i, 1] for i in range(27)], axis=0)
    narrow = ((iota((128, 128), 0) >> 1) == iota((128, 128), 1)).astype(jnp.float32)
    down, across = iota((216, 216), 0), iota((216, 216), 1)
    low = ((down >> 3) == (across >> 3)) & (((across & 7) >> 1) == (down & 7))
    mean = 0.125 * dot(low.astype(jnp.float32), dot(pair, narrow))
    settled = interface([mean[8 * i : 8 * i + 8] for i in range(27)], restrict_factor)
    for j in range(9):
        rs[j] = settled[DOWN[0][j]]
    for way in (1, -1):
        face = h if way > 0 else 1 - h
        depths, coarse_depths = ((7, 6, 5), (3, 2)) if way > 0 else ((0, 1, 2), (0, 1))
        inward = UP[1] if way > 0 else DOWN[1]
        for x in range(4):

            def put(base, k, ref, depth):
                at = 4 * (k % 2) + x
                value = ref[depth : depth + 1, :].astype(jnp.float32)
                faces[face, base + k // 2, at : at + 1, :] = value

            for ch in range(27):
                put(0, ch, pop.at[ch, x], depths[0])
            put(0, 27, mask.at[x], depths[0])
            for k in range(9):
                put(T_DEEP, k, pop.at[inward[k], x], depths[1])
            for k in range(4):
                put(T_DEEP, 9 + k, mom.at[k, x], depths[1])
            put(T_DEEP, 13, mask.at[x], depths[1])
            for k in range(3):
                put(T_DEEP, 14 + k, vel.at[k, x], depths[2])
        r = coarse_depths[0]
        for j, i in enumerate(inward):
            lane = 64 * (j // 5)
            for x in range(8):
                faces[face, T_COARSE + j % 5, x : x + 1, lane : lane + 64] = cc[x, i, r : r + 1, 0:64]
        for (ch, depth), (tile, at, lane) in LEVEL[way].items():
            r = coarse_depths[depth]
            if ch < 27:
                value = rc[ch, 7, r : r + 1, 0:64]
            elif ch < 36:
                value = cc[6, UP[0][ch - 27], r : r + 1, 0:64]
            elif ch < 45:
                value = rs[ch - 36, r : r + 1, 0:64]
            else:
                value = inflow[r : r + 1, :]
            faces[face, tile, at : at + 1, lane : lane + 64] = value
    near[0:T_FACE] = faces[0]
    far[...] = faces[1]


def particle_fields(rows):
    lane = iota((2, 128), 1) >> 5
    chunks = [[] for _ in range(4)]
    for k in range(4):
        turned = [[roll(rows[4 * k + j], 32 * s, 1) for s in range(4)] for j in range(4)]
        for q in range(4):
            value = turned[0][(0 - q) % 4]
            for j in range(1, 4):
                value = jnp.where(lane == j, turned[j][(j - q) % 4], value)
            chunks[q].append(value)
    flat = [jnp.concatenate(chunks[q], axis=1) for q in range(4)]
    return [flat[f % 4][f // 4 : f // 4 + 1, :] for f in range(8)]


def deposit(fields, velocity, xr, yr, keep):
    rows = velocity[0].shape[0]
    count = fields[0].shape[1]
    cell = fields[7].astype(jnp.int32)
    ix, iy, iz = cell >> 10, (cell >> 7) & 7, cell & 127
    fx, fy, fz = fields[4:7]
    lane = iota((128, count), 0)
    along = jnp.where(lane == iz, 1.0 - fz, jnp.where(lane == iz + 1, fz, 0.0))
    across = jnp.where(xr == ix, 1.0 - fx, jnp.where(xr == ix + 1, fx, 0.0))
    across = across * jnp.where(yr == iy, 1.0 - fy, jnp.where(yr == iy + 1, fy, 0.0))
    seen = dot(jnp.concatenate(velocity, axis=0), along)
    pushes = []
    for k in range(3):
        sampled = jnp.sum(seen[k * rows : (k + 1) * rows] * across, axis=0, keepdims=True)
        impulse = fields[3] * (fields[k] - sampled)
        pushes.append(impulse * across[0:keep])
    force = dot(jnp.concatenate(pushes, axis=0), along, (1, 1))
    return [force[k * keep : (k + 1) * keep] for k in range(3)]


def choose(sc, near, fwd):
    lower = sc[S_H] == 0
    return (lambda t: jnp.where(lower, near[t], fwd[t])), (lambda t: jnp.where(lower, fwd[t], near[t]))


def level_kernel(sc, cc, r127, rs, inflow, near, fwd, sw, inf, hi, lo):
    up, down = choose(sc, near, fwd)
    for t in range(22, T_FACE):
        hi[t], lo[t] = up(t), down(t)
    for t in range(T_SW):
        sw[t] = jnp.zeros((8, 128), jnp.float32)
    inf[...] = jnp.zeros((8, 128), jnp.float32)
    inf[0:4, 0:64] = inflow[...]

    def halo(ch, ref, to):
        for face, way, rows in ((hi, -1, (4, 5)), (lo, 1, (7, 6))):
            for depth in range(2):
                spot = LEVEL[way].get((ch, depth))
                if spot is not None:
                    tile, at, lane = spot
                    r = rows[depth]
                    ref[r : r + 1, to : to + 64] = face[tile, at : at + 1, lane : lane + 64]

    halo(45, inf, 0)

    @pl.when(sc[S_FIRST] == 1)
    def _():
        for j in range(9):
            to = 64 * (j % 2)
            sw[j // 2, 0:4, to : to + 64] = rs[j, 0:4, 0:64]
            halo(36 + j, sw.at[j // 2], to)

    @pl.when(sc[S_FIRST] == 0)
    def _():
        for ch in range(36):
            to = 64 * (ch % 2)
            own = r127.at[ch] if ch < 27 else cc.at[6, UP[0][ch - 27]]
            sw[ch // 2, 0:4, to : to + 64] = own[0:4, 0:64]
            halo(ch, sw.at[ch // 2], to)


def deposit_kernel(sc, pop, mask, vel, cc, near, fwd, arr, third_in, ye, xa, xb, ccy, hi, lo):
    h = sc[S_H]
    lower = h == 0
    up, down = choose(sc, near, fwd)
    for t in range(T_FACE):
        hi[t], lo[t] = up(t), down(t)
    own = particle_fields([arr[2 * s + h] for s in range(16)])
    partner = particle_fields([arr[2 * s + 1 - h] for s in range(16)])
    third = particle_fields([third_in[s // 4, 2 * (s % 4) : 2 * (s % 4) + 2, :] for s in range(16)])
    high = [jnp.where(lower, a, b) for a, b in zip(partner, third)]
    low = [jnp.where(lower, b, a) for a, b in zip(partner, third)]
    rows32 = iota((32, 1), 0)
    force = deposit(
        own,
        [jnp.concatenate([vel[k, x] for x in range(4)], axis=0) for k in range(3)],
        rows32 >> 3,
        rows32 & 7,
        32,
    )
    row = iota((8, 128), 0)
    first_half = row < 4

    def layer(base, k):
        a, b = hi[base + k // 2], lo[base + k // 2]
        return jnp.where(first_half, roll(a, 4, 0), b) if k % 2 else jnp.where(first_half, a, roll(b, 4, 0))

    n1 = [layer(0, ch) for ch in range(27)]
    g1 = layer(0, 27)
    n2 = [layer(T_DEEP, k) for k in range(9)]
    density2, m2, g2 = layer(T_DEEP, 9), [layer(T_DEEP, 10 + k) for k in range(3)], layer(T_DEEP, 13)
    v3 = [layer(T_DEEP, 14 + k) for k in range(3)]
    density1, m1 = moments(n1)
    inverse1, inverse2 = 1.0 / (density1 + (1.0 - g1)), 1.0 / (density2 + (1.0 - g2))
    rows16 = iota((16, 1), 0)
    pushed = []
    for above, fields in ((True, high), (False, low)):
        velocity = []
        for k in range(3):
            a, b = m1[k] * inverse1, m2[k] * inverse2
            c = jnp.where(first_half, v3[k] if above else roll(v3[k], 4, 0), 0.0)
            ab = jnp.where(first_half, a, roll(b, 4, 0)) if above else jnp.where(first_half, roll(a, 4, 0), b)
            velocity.append(jnp.concatenate([ab, c], axis=0))
        depth = rows16 >> 2
        pushed.append(deposit(fields, velocity, rows16 & 3, depth if above else 7 - depth, 8))
    f1 = [jnp.where(first_half, a, roll(b, 4, 0)) for a, b in zip(*pushed)]
    f2 = [jnp.where(first_half, roll(a, 4, 0), b) for a, b in zip(*pushed)]
    side1 = collide(n1, g1, f1, tau_fine) + [g1] + f1
    s2 = density2 + (1.0 - g2)
    u2 = [(m2[k] + tau_fine * f2[k]) * inverse2 for k in range(3)]
    u2[1] = jnp.where(first_half, u2[1], -u2[1])
    e2 = equilibrium(s2 * (1.0 / tau_fine), u2)
    side2 = [
        jnp.where(g2 > 0.0, (1.0 - 1.0 / tau_fine) * n2[k] + e2[DOWN[1][k]], wall) for k in range(9)
    ]
    for x in range(4):
        g = mask[x].astype(jnp.float32)
        f = [force[k][8 * x : 8 * x + 8] for k in range(3)]
        mine = collide([pop[i, x] for i in range(27)], g, f, tau_fine) + [g] + f
        for ch in range(31):
            ye[x, ch, 0:8, :] = mine[ch]
            value = jnp.where(row == 0, roll(side1[ch], -x, 0), 0.0)
            value = jnp.where(row == 7, roll(side1[ch], 3 - x, 0), value)
            if ch in DOWN[1]:
                value = jnp.where(row == 1, roll(side2[DOWN[1].index(ch)], 1 - x, 0), value)
            if ch in UP[1]:
                value = jnp.where(row == 6, roll(side2[UP[1].index(ch)], 2 - x, 0), value)
            ye[x, ch, 8:16, :] = value
    ccy[...] = cc[...]
    has_hi, has_lo = sc[S_YHI] == 1, sc[S_YLO] == 1
    for face, way, has, r in ((hi, DOWN[1], has_hi, 4), (lo, UP[1], has_lo, 7)):
        for j, i in enumerate(way):
            lane = 64 * (j // 5)
            for x in range(8):
                value = face[T_COARSE + j % 5, x : x + 1, lane : lane + 64]
                ccy[x, i, r : r + 1, 0:64] = jnp.where(has, value, wall)
    even = sc[S_CORE] == 0
    outer = (row < 2) | (row >= 6)

    def send(t, a, b):
        xa[t], xb[t] = jnp.where(even, a, b), jnp.where(even, b, a)

    ups = [(3, ch) for ch in range(31)] + [(2, i) for i in UP[0]]
    downs = [(0, ch) for ch in range(31)] + [(1, i) for i in DOWN[0]]
    for k in range(40):
        send(k, ye[ups[k] + (slice(0, 8),)], ye[downs[k] + (slice(0, 8),)])
    for k in range(20):
        pairs = []
        for which in (ups, downs):
            first, second = which[2 * k], which[2 * k + 1]
            value = roll(ye[second + (slice(8, 16),)], 4, 0)
            pairs.append(jnp.where(outer, ye[first + (slice(8, 16),)], value))
        send(X_ROWS + k, *pairs)
    for j in range(9):
        send(X_COARSE + j, ccy[7, UP[0][j]], ccy[0, DOWN[0][j]])


def x_tile(ye, up, down, x, ch):
    if 2 <= x <= 5:
        return ye[x - 2, ch]
    face = down if x < 2 else up
    slot = ch if x in (1, 6) else 31 + (UP[0] if x == 0 else DOWN[0]).index(ch)
    row = iota((8, 128), 0)
    rest = roll(face(X_ROWS + slot // 2), 4 * (slot % 2), 0)
    return jnp.concatenate([face(slot), jnp.where((row < 2) | (row >= 6), rest, 0.0)], axis=0)


def pick(sc, index, a, b):
    even = sc[index] == 0
    return (lambda t: jnp.where(even, a[t], b[t])), (lambda t: jnp.where(even, b[t], a[t]))


def column_kernel(sc, ye, xar, xbr, swr, ccy, sw, inf, za, zb):
    up, down = pick(sc, S_CORE, xar, xbr)
    lane = iota((16, 128), 1)
    lane8 = iota((8, 128), 1)
    made = {}
    for way in (1, -1):
        tiles = [jnp.zeros((16, 128), jnp.float32) for _ in range(3)]
        for (depth, x, ch), spot in ZL[way].items():
            source = 127 - depth if way > 0 else depth
            value = roll(x_tile(ye, up, down, x, ch), spot - source, 1)
            tiles[spot // 128] = jnp.where(lane == spot % 128, value, tiles[spot // 128])
        out = [t[8 * k : 8 * k + 8] for t in tiles for k in range(2)]
        tiles = [jnp.zeros((8, 128), jnp.float32) for _ in range(2)]
        for item, spot in CL[way].items():
            if item[0] == "c":
                _, x, i = item
                if x == 0:
                    value = down(X_COARSE + UP[0].index(i))
                elif x == 9:
                    value = up(X_COARSE + DOWN[0].index(i))
                else:
                    value = ccy[x - 1, i]
                source = 63 if way > 0 else 0
            elif item[0] == "g":
                _, ch, depth = item
                q = ch if ch < 36 else ch - 36
                value = swr[q // 2] if ch < 36 else sw[q // 2]
                source = (63 - depth if way > 0 else depth) + 64 * (q % 2)
            else:
                value = inf[...]
                source = 63 if way > 0 else 0
            value = roll(value, spot - source, 1)
            tiles[spot // 128] = jnp.where(lane8 == spot % 128, value, tiles[spot // 128])
        made[way] = out + tiles
    even = sc[S_ODD] == 0
    for t in range(8):
        za[t] = jnp.where(even, made[1][t], made[-1][t])
        zb[t] = jnp.where(even, made[-1][t], made[1][t])


def step_kernel(
    sc, ye, xar, xbr, swr, ccy, sw, inf, zar, zbr, fine, coarse, p1, p2, gx, fx, ce, gr, late
):
    up, down = pick(sc, S_CORE, xar, xbr)
    zup, zdown = pick(sc, S_ODD, zar, zbr)
    has_yhi, has_ylo, has_zhi, has_zlo = [sc[k] == 1 for k in (S_YHI, S_YLO, S_ZHI, S_ZLO)]
    first, last = sc[S_FIRST] == 1, sc[S_LAST] == 1
    fz_up = [jnp.concatenate([zup(2 * k), zup(2 * k + 1)], axis=0) for k in range(3)]
    fz_down = [jnp.concatenate([zdown(2 * k), zdown(2 * k + 1)], axis=0) for k in range(3)]
    cz_up, cz_down = [zup(6), zup(7)], [zdown(6), zdown(7)]
    lane = iota((16, 128), 1)
    lane8 = iota((8, 128), 1)

    def side(x, ch):
        blank = wall if ch < 27 else 0.0
        value = jnp.zeros((16, 128), jnp.float32)
        for depth in range(2):
            for way, source, has, at in ((-1, fz_up, has_zhi, depth), (1, fz_down, has_zlo, 127 - depth)):
                spot = ZL[way].get((depth, x, ch))
                if spot is not None:
                    moved = jnp.where(has, roll(source[spot // 128], at - spot, 1), blank)
                    value = jnp.where(lane == at, moved, value)
        return value

    for x in range(8):
        for ch in range(31) if 0 < x < 7 else (UP[0] if x == 0 else DOWN[0]):
            main, rest = x_tile(ye, up, down, x, ch), side(x, ch)
            if ch < 27:
                to = p1.at[x, ch]
            elif ch == 27:
                to = gx.at[x - 1]
            else:
                to = fx.at[x - 1, ch - 28]
            to[:, 0:128] = main
            to[:, 128:256] = rest

    row8 = iota((8, 128), 0)
    inside = (row8 < 4) | ((row8 < 6) & has_yhi) | ((row8 >= 6) & has_ylo)
    inside = inside & (
        (lane8 < 64) | ((lane8 >= 64) & (lane8 < 66) & has_zhi) | ((lane8 >= 126) & has_zlo)
    )

    def c_side(value, up_item, down_item, blank, at=64, end=127):
        for way, source, has, item, to in ((-1, cz_up, has_zhi, up_item, at), (1, cz_down, has_zlo, down_item, end)):
            spot = CL[way].get(item)
            if spot is not None:
                moved = jnp.where(has, roll(source[spot // 128], to - spot, 1), blank)
                value = jnp.where(lane8 == to, moved, value)
        return value

    def ghost(ch, ref, q):
        value = roll(ref[q // 2], 64 * (q % 2), 1)
        value = jnp.where(lane8 < 64, value, 0.0)
        for depth in range(2):
            item = ("g", ch, depth)
            value = c_side(value, item, item, 0.0, 64 + depth, 127 - depth)
        return value

    for x in range(8):
        for i in range(27):
            ce[x + 1, i] = c_side(ccy[x, i], ("c", x + 1, i), ("c", x + 1, i), wall)
    inflow = c_side(inf[...], ("i",), ("i",), 0.0)
    zero = jnp.zeros((8, 128), jnp.float32)
    inlet = equilibrium(jnp.ones((8, 128), jnp.float32), [inflow, zero, zero])
    for j in range(9):
        i = UP[0][j]
        came = c_side(down(X_COARSE + j), ("c", 0, i), ("c", 0, i), wall)
        ce[0, i] = jnp.where(first, jnp.where(inside, inlet[i], wall), came)
        i = DOWN[0][j]
        came = c_side(up(X_COARSE + j), ("c", 9, i), ("c", 9, i), wall)
        ce[9, i] = jnp.where(last, jnp.where(inside, ghost(j, swr, j), wall), came)
    for i in range(27):
        a, b, c = stencil[i]
        for x in range(8):
            value = roll(roll(ce[x + 1 - a, i], b, 0), c, 1)
            value = jnp.where(value > limit, value, ce[x + 1, 26 - i])
            coarse[i, x] = value[0:4, 0:64]

    @pl.when(first)
    def _():
        n127 = [ghost(i, swr, i) for i in range(27)]
        post = collide(n127, None, None, tau_coarse)
        for i in range(27):
            gr[1, i] = jnp.where(inside, post[i], wall)
        for j in range(9):
            gr[0, UP[0][j]] = jnp.where(inside, ghost(27 + j, swr, 27 + j), wall)
            gr[2, DOWN[0][j]] = jnp.where(inside, ghost(36 + j, sw, j), wall)
        later = []
        for i in range(27):
            a, b, c = stencil[i]
            value = roll(roll(gr[1 - a, i], b, 0), c, 1)
            value = jnp.where(value > limit, value, gr[1, 26 - i])
            later.append(jnp.where(inside, 0.5 * (n127[i] + value), 0.0))
        wide = ((iota((128, 256), 1) >> 1) == iota((128, 256), 0)).astype(jnp.float32)
        tall = ((iota((432, 216), 0) >> 1) == iota((432, 216), 1)).astype(jnp.float32)
        row16, lane256 = iota((16, 256), 0), iota((16, 256), 1)
        within = (row16 < 8) | ((row16 < 12) & has_yhi) | ((row16 >= 12) & has_ylo)
        within = within & (
            (lane256 < 128) | ((lane256 < 132) & has_zhi) | ((lane256 >= 252) & has_zlo)
        )
        for layer, to in ((n127, p1.at[1]), (later, late)):
            layer = interface(layer, prolong_factor)
            fines = dot(tall, dot(jnp.concatenate(layer, axis=0), wide))
            for i in range(27):
                to[i] = jnp.where(within, fines[16 * i : 16 * i + 16], wall)

    @pl.when(last)
    def _():
        for i in range(27):
            p1[6, i] = p1[5, i]

    def stream_layer(m, carry):
        g = gx[m]
        for i in range(27):
            a, b, c = stencil[i]
            value = roll(roll(p1[m + 1 - a, i], b, 0), c, 1)
            value = jnp.where(value > limit, value, p1[m + 1, 26 - i])
            p2[m, i] = jnp.where(g > 0.0, value, 0.0)
        return carry

    lax.fori_loop(0, 6, stream_layer, 0)

    def collide_layer(m, carry):
        for y in range(2):
            for z in range(2):
                rows, lanes = slice(8 * y, 8 * y + 8), slice(128 * z, 128 * z + 128)
                post = collide(
                    [p2[m, i, rows, lanes] for i in range(27)],
                    gx[m, rows, lanes],
                    [fx[m, k, rows, lanes] for k in range(3)],
                    tau_fine,
                )
                for i in range(27):
                    p2[m, i, rows, lanes] = post[i]
        return carry

    lax.fori_loop(0, 6, collide_layer, 0)

    @pl.when(first)
    def _():
        for i in range(27):
            p2[0, i] = late[i]

    @pl.when(last)
    def _():
        for i in range(27):
            p2[5, i] = p2[4, i]

    def finish_layer(x, carry):
        g = gx[x + 1, 0:8, 0:128]
        for i in range(27):
            a, b, c = stencil[i]
            value = roll(roll(p2[x + 1 - a, i], b, 0), c, 1)[0:8, 0:128]
            value = jnp.where(value > limit, value, p2[x + 1, 26 - i, 0:8, 0:128])
            fine[i, x] = jnp.where(g > 0.0, value, 0.0)
        return carry

    lax.fori_loop(0, 4, finish_layer, 0)


def f32(*shape):
    return jax.ShapeDtypeStruct(shape, jnp.float32)


def call(kernel, name, out_shape, scratch, *args, held=0, cost=0):
    vmem = pl.BlockSpec(memory_space=pltpu.VMEM)
    raw = pl.BlockSpec(memory_space=pltpu.HBM)
    return pl.pallas_call(
        kernel,
        out_shape=out_shape,
        in_specs=[pl.BlockSpec(memory_space=pltpu.SMEM)] + [raw] * held + [vmem] * (len(args) - 1 - held),
        out_specs=[vmem] * len(out_shape),
        scratch_shapes=[pltpu.VMEM(s, jnp.float32) for s in scratch]
        + ([pltpu.SemaphoreType.DMA((held,))] if held else []),
        compiler_params=pltpu.CompilerParams(vmem_limit_bytes=40 * 1024 * 1024),
        cost_estimate=pl.CostEstimate(flops=cost, bytes_accessed=1, transcendentals=0) if cost else None,
        name=name,
    )(*args)


def body(pop, cpop, mask, inflow, part_dest, part_cell, part_vel, part_frac, part_drag):
    gx, gy, h, gz = [lax.axis_index(a) for a in ("gx", "y", "h", "gz")]
    n_gx, n_y, n_gz = lax.axis_size("gx"), lax.axis_size("y"), lax.axis_size("gz")
    row = gy * 2 + h
    sc = jnp.stack(
        [
            h,
            gx % 2,
            gz % 2,
            (gx == 0).astype(jnp.int32),
            (gx == n_gx - 1).astype(jnp.int32),
            (row > 0).astype(jnp.int32),
            (row < 2 * n_y - 1).astype(jnp.int32),
            (gz > 0).astype(jnp.int32),
            (gz < n_gz - 1).astype(jnp.int32),
        ]
    ).astype(jnp.int32)
    far, near, vel, cc, r127, rs = call(
        pack_kernel,
        "pack",
        [
            f32(T_FACE, 8, 128),
            f32(T_FACE + 1, 8, 128),
            f32(3, 4, 8, 128),
            f32(8, 27, 8, 128),
            f32(27, 8, 128),
            f32(9, 8, 128),
        ],
        [(27, 4, 8, 128), (27, 8, 4, 64), (27, 8, 8, 128), (4, 4, 8, 128), (2, T_FACE, 8, 128)],
        sc,
        pop,
        cpop,
        mask,
        inflow,
        held=2,
        cost=1_000_000_000,
    )
    (outbox,) = call(
        route_kernel,
        "route",
        [f32(64, 128)],
        [],
        sc,
        part_dest.reshape(1, 256),
        part_cell.reshape(1, 256),
        part_vel,
        part_frac,
        part_drag.reshape(1, 256),
        rs,
        cost=50_000_000_000,
    )
    far = lax.ppermute(far, "h", [(0, 1), (1, 0)])
    arr = lax.all_to_all(outbox.reshape(2 * n_gx, 2, 128), ("gx", "h"), 0, 0, tiled=True)
    near = lax.ppermute(near, "h", [(0, 1), (1, 0)])
    onward = [(2 * y, 2 * y + 2) for y in range(n_y - 1)]
    onward += [(2 * y + 3, 2 * y + 1) for y in range(n_y - 1)]
    partner = jnp.where(h == 0, arr[1::2], arr[0::2]).reshape(4, 8, 128)
    fwd = lax.ppermute(far, ("y", "h"), onward)
    third = lax.ppermute(partner, ("y", "h"), onward)
    sw, inf = call(
        level_kernel,
        "level",
        [f32(T_X + 1, 8, 128), f32(8, 128)],
        [(T_FACE, 8, 128), (T_FACE, 8, 128)],
        sc,
        cc,
        r127,
        rs,
        inflow,
        near,
        fwd,
    )
    swr = lax.ppermute(sw, "gx", [(0, n_gx - 1), (n_gx - 1, 0)])
    ye, xa, xb, ccy = call(
        deposit_kernel,
        "deposit",
        [f32(4, 31, 16, 128), f32(T_X, 8, 128), f32(T_X, 8, 128), f32(8, 27, 8, 128)],
        [(T_FACE, 8, 128), (T_FACE, 8, 128)],
        sc,
        pop,
        mask,
        vel,
        cc,
        near,
        fwd,
        arr,
        third,
        cost=50_000_000_000,
    )
    xar = lax.ppermute(xa, "gx", [(i, i ^ 1) for i in range(n_gx)])
    inner = [(i, i + 1) for i in range(1, n_gx - 1, 2)]
    xbr = lax.ppermute(xb, "gx", inner + [(j, i) for i, j in inner])
    za, zb = call(
        column_kernel,
        "columns",
        [f32(8, 8, 128), f32(8, 8, 128)],
        [],
        sc,
        ye,
        xar,
        xbr,
        swr,
        ccy,
        sw,
        inf,
    )
    zar = lax.ppermute(za, "gz", [(i, i ^ 1) for i in range(n_gz)])
    inner = [(i, i + 1) for i in range(1, n_gz - 1, 2)]
    zbr = lax.ppermute(zb, "gz", inner + [(j, i) for i, j in inner])
    fine, coarse = call(
        step_kernel,
        "steps",
        [f32(27, 4, 8, 128), f32(27, 8, 4, 64)],
        [
            (8, 27, 16, 256),
            (6, 27, 16, 256),
            (6, 16, 256),
            (6, 3, 16, 256),
            (10, 27, 8, 128),
            (3, 27, 8, 128),
            (27, 16, 256),
        ],
        sc,
        ye,
        xar,
        xbr,
        swr,
        ccy,
        sw,
        inf,
        zar,
        zbr,
    )
    return fine, coarse


def solution(mesh):
    n_gx, n_gy, n_gz = [mesh.shape[a] for a in ("gx", "gy", "gz")]
    split = Mesh(mesh.devices.reshape(n_gx, n_gy // 2, 2, n_gz), ("gx", "y", "h", "gz"))
    gy = ("y", "h")
    return jax.shard_map(
        body,
        mesh=split,
        in_specs=(
            P(None, "gx", gy, "gz"),
            P(None, "gx", gy, "gz"),
            P("gx", gy, "gz"),
            P(gy, "gz"),
            P("gx", gy, "gz", None, None),
            P("gx", gy, "gz", None),
            P("gx", gy, "gz", None, None),
            P("gx", gy, "gz", None, None),
            P("gx", gy, "gz", None),
        ),
        out_specs=(P(None, "gx", gy, "gz"), P(None, "gx", gy, "gz")),
        check_vma=False,
    )
```

```python
import jax
import jax.numpy as jnp
from jax import lax
from jax.experimental import pallas as pl
from jax.experimental.pallas import tpu as pltpu
from jax.sharding import Mesh, PartitionSpec as P

tau_fine = 1.3
tau_coarse = 0.9
prolong_factor = (tau_fine - 1.0) / (2.0 * tau_coarse)
restrict_factor = 2.0 * (tau_coarse - 1.0) / tau_fine
stencil = [(a, b, c) for a in (-1, 0, 1) for b in (-1, 0, 1) for c in (-1, 0, 1)]
class_weight = (8.0 / 27.0, 2.0 / 27.0, 1.0 / 54.0, 1.0 / 216.0)
wall = -1e30
limit = -1e29


def moving(axis, way):
    return [i for i in range(27) if stencil[i][axis] == way]


UP = [moving(axis, 1) for axis in range(3)]
DOWN = [moving(axis, -1) for axis in range(3)]

T_DEEP, T_COARSE, T_LEVEL, T_FACE = 14, 23, 22, 33
X_ROWS, X_COARSE, T_X = 40, 60, 69


def level_rows():
    rows = [(ch, 0) for ch in range(46)] + [(ch, 1) for ch in range(45)]
    spots = [(22, r, 64 * half) for r in range(4, 8) for half in range(2)]
    spots += [(27, r, 64) for r in range(8)]
    spots += [(t, r, 64 * half) for t in range(28, 33) for r in range(8) for half in range(2)]
    return dict(zip(rows, spots))


LEVEL = level_rows()
T_SW = 18

z_items = [(0, x, ch) for x in range(1, 7) for ch in range(31)]
z_items += [(0, 0, i) for i in UP[0]] + [(0, 7, i) for i in DOWN[0]]
z_deep = [(1, x, j) for x in range(1, 7) for j in range(9)]


def z_layout(way):
    inward = UP[2] if way > 0 else DOWN[2]
    items = list(z_items) + [(1, x, inward[j]) for (_, x, j) in z_deep]
    items += [(1, 0, i) for i in inward if stencil[i][0] == 1]
    items += [(1, 7, i) for i in inward if stencil[i][0] == -1]
    return {item: spot for spot, item in enumerate(items)}


def c_layout(way):
    inward = UP[2] if way > 0 else DOWN[2]
    items = [("c", x, i) for x in range(1, 9) for i in inward]
    items += [("c", 0, i) for i in inward if stencil[i][0] == 1]
    items += [("c", 9, i) for i in inward if stencil[i][0] == -1]
    items += [("g", ch, 0) for ch in range(45)] + [("g", ch, 1) for ch in range(27)]
    items += [("g", 27 + j, 1) for j in range(9) if stencil[UP[0][j]][2] == way]
    items += [("g", 36 + j, 1) for j in range(9) if stencil[DOWN[0][j]][2] == way]
    items += [("i",)]
    return {item: spot for spot, item in enumerate(items)}


ZL = {1: z_layout(1), -1: z_layout(-1)}
CL = {1: c_layout(1), -1: c_layout(-1)}


def roll(value, by, axis):
    by = by % value.shape[axis]
    return value if by == 0 else pltpu.roll(value, by, axis)


def iota(shape, axis):
    return lax.broadcasted_iota(jnp.int32, shape, axis)


def dot(a, b, contract=(1, 0)):
    return lax.dot_general(
        a,
        b,
        (((contract[0],), (contract[1],)), ((), ())),
        precision=lax.Precision.HIGHEST,
        preferred_element_type=jnp.float32,
    )


def moments(n):
    totals = [n[13], None, None, None]
    parts = [[None] * 4 for _ in range(3)]
    for i in range(14, 27):
        c = stencil[i]
        k = abs(c[0]) + abs(c[1]) + abs(c[2])
        both, odd = n[i] + n[26 - i], n[i] - n[26 - i]
        totals[k] = both if totals[k] is None else totals[k] + both
        for axis in range(3):
            if c[axis]:
                have = parts[axis][k]
                if have is None:
                    parts[axis][k] = odd if c[axis] > 0 else -odd
                else:
                    parts[axis][k] = have + odd if c[axis] > 0 else have - odd
    density = sum(class_weight[k] * totals[k] for k in range(4))
    momentum = [sum(class_weight[k] * parts[axis][k] for k in (1, 2, 3)) for axis in range(3)]
    return density, momentum


def equilibrium(s, u):
    base = s - (1.5 * (u[0] * u[0] + u[1] * u[1] + u[2] * u[2])) * s
    s3, s45 = 3.0 * s, 4.5 * s
    out = [None] * 27
    out[13] = base
    for i in range(14, 27):
        cu = None
        for axis in range(3):
            c = stencil[i][axis]
            if c:
                if cu is None:
                    cu = u[axis] if c > 0 else -u[axis]
                else:
                    cu = cu + u[axis] if c > 0 else cu - u[axis]
        even, odd = base + s45 * (cu * cu), s3 * cu
        out[i], out[26 - i] = even + odd, even - odd
    return out


def collide(n, g, force, tau):
    density, m = moments(n)
    s = jnp.where(density == 0.0, 1.0, density) if g is None else density + (1.0 - g)
    inverse = 1.0 / s
    if force is not None:
        m = [m[k] + tau * force[k] for k in range(3)]
    e = equilibrium(s * (1.0 / tau), [v * inverse for v in m])
    post = [(1.0 - 1.0 / tau) * n[i] + e[i] for i in range(27)]
    return post if g is None else [jnp.where(g > 0.0, p, wall) for p in post]


def interface(n, factor):
    density, m = moments(n)
    density = jnp.where(density == 0.0, 1.0, density)
    inverse = 1.0 / density
    e = equilibrium(density, [v * inverse for v in m])
    return [e[i] + factor * (n[i] - e[i]) for i in range(27)]


S_H, S_CORE, S_ODD, S_FIRST, S_LAST, S_YLO, S_YHI, S_ZLO, S_ZHI = range(9)


def route_kernel(sc, pdest, pcell, pvel, pfrac, pdrag, anchor, outbox):
    del sc, anchor
    dest = pdest[...]
    onehot = (iota((16, 256), 0) == dest).astype(jnp.float32)
    earlier = (iota((256, 256), 0) < iota((256, 256), 1)).astype(jnp.bfloat16)
    before = jnp.dot(onehot.astype(jnp.bfloat16), earlier, preferred_element_type=jnp.float32)
    rank = jnp.sum(onehot * before, axis=0, keepdims=True).astype(jnp.int32)
    slot = (iota((32, 256), 0) == rank).astype(jnp.float32)
    row = iota((64, 256), 0)
    hit = (row >> 2) == dest
    odd = (row & 1) == 1
    fields = [pvel[0, 0, 0, k : k + 1, :] for k in range(3)] + [pdrag[...]]
    fields += [pfrac[0, 0, 0, k : k + 1, :] for k in range(3)] + [pcell[...].astype(jnp.float32)]
    for q in range(4):
        values = jnp.where(hit, jnp.where(odd, fields[4 + q], fields[q]), 0.0)
        outbox[:, 32 * q : 32 * q + 32] = dot(values, slot, (1, 1))


def pack_kernel(
    sc, pop, cpop, mask, inflow, faces, vel, cc, r127, rs, rc, mom,
):
    h = sc[S_H]
    rc[...] = jnp.zeros(rc.shape, jnp.float32)
    faces[...] = jnp.zeros(faces.shape, jnp.float32)
    for x in range(4):
        density, m = moments([pop[i, x] for i in range(27)])
        inverse = 1.0 / (density + (1.0 - mask[x].astype(jnp.float32)))
        mom[0, x] = density
        for k in range(3):
            mom[k + 1, x] = m[k]
            vel[k, x] = m[k] * inverse
    for i in range(27):
        rc[i, :, 0:4, 0:64] = cpop[i]
        r127[i] = rc[i, 7]
    for x in range(8):
        post = collide([rc[i, x] for i in range(27)], None, None, tau_coarse)
        for i in range(27):
            cc[x, i] = post[i]
    pair = jnp.concatenate([pop[i, 0] + pop[i, 1] for i in range(27)], axis=0)
    narrow = ((iota((128, 128), 0) >> 1) == iota((128, 128), 1)).astype(jnp.float32)
    down, across = iota((216, 216), 0), iota((216, 216), 1)
    low = ((down >> 3) == (across >> 3)) & (((across & 7) >> 1) == (down & 7))
    mean = 0.125 * dot(low.astype(jnp.float32), dot(pair, narrow))
    settled = interface([mean[8 * i : 8 * i + 8] for i in range(27)], restrict_factor)
    for j in range(9):
        rs[j] = settled[DOWN[0][j]]
    for way in (1, -1):
        face = h if way > 0 else 1 - h
        depths, coarse_depths = ((7, 6, 5), (3, 2)) if way > 0 else ((0, 1, 2), (0, 1))
        inward = UP[1] if way > 0 else DOWN[1]
        for x in range(4):

            def put(base, k, ref, depth):
                at = 4 * (k % 2) + x
                value = ref[depth : depth + 1, :].astype(jnp.float32)
                faces[face, base + k // 2, at : at + 1, :] = value

            for ch in range(27):
                put(0, ch, pop.at[ch, x], depths[0])
            put(0, 27, mask.at[x], depths[0])
            for k in range(9):
                put(T_DEEP, k, pop.at[inward[k], x], depths[1])
            for k in range(4):
                put(T_DEEP, 9 + k, mom.at[k, x], depths[1])
            put(T_DEEP, 13, mask.at[x], depths[1])
            for k in range(3):
                put(T_DEEP, 14 + k, vel.at[k, x], depths[2])
        r = coarse_depths[0]
        for j, i in enumerate(inward):
            lane = 64 * (j // 5)
            for x in range(8):
                faces[face, T_COARSE + j % 5, x : x + 1, lane : lane + 64] = cc[x, i, r : r + 1, 0:64]
        for (ch, depth), (tile, at, lane) in LEVEL.items():
            r = coarse_depths[depth]
            if ch < 27:
                value = rc[ch, 7, r : r + 1, 0:64]
            elif ch < 36:
                value = cc[6, UP[0][ch - 27], r : r + 1, 0:64]
            elif ch < 45:
                value = rs[ch - 36, r : r + 1, 0:64]
            else:
                value = inflow[r : r + 1, :]
            faces[face, tile, at : at + 1, lane : lane + 64] = value


def particle_fields(rows):
    lane = iota((2, 128), 1) >> 5
    chunks = [[] for _ in range(4)]
    for k in range(4):
        turned = [[roll(rows[4 * k + j], 32 * s, 1) for s in range(4)] for j in range(4)]
        for q in range(4):
            value = turned[0][(0 - q) % 4]
            for j in range(1, 4):
                value = jnp.where(lane == j, turned[j][(j - q) % 4], value)
            chunks[q].append(value)
    flat = [jnp.concatenate(chunks[q], axis=1) for q in range(4)]
    return [flat[f % 4][f // 4 : f // 4 + 1, :] for f in range(8)]


def deposit(fields, velocity, xr, yr, keep):
    rows = velocity[0].shape[0]
    count = fields[0].shape[1]
    cell = fields[7].astype(jnp.int32)
    ix, iy, iz = cell >> 10, (cell >> 7) & 7, cell & 127
    fx, fy, fz = fields[4:7]
    lane = iota((128, count), 0)
    along = jnp.where(lane == iz, 1.0 - fz, jnp.where(lane == iz + 1, fz, 0.0))
    across = jnp.where(xr == ix, 1.0 - fx, jnp.where(xr == ix + 1, fx, 0.0))
    across = across * jnp.where(yr == iy, 1.0 - fy, jnp.where(yr == iy + 1, fy, 0.0))
    seen = dot(jnp.concatenate(velocity, axis=0), along)
    pushes = []
    for k in range(3):
        sampled = jnp.sum(seen[k * rows : (k + 1) * rows] * across, axis=0, keepdims=True)
        impulse = fields[3] * (fields[k] - sampled)
        pushes.append(impulse * across[0:keep])
    force = dot(jnp.concatenate(pushes, axis=0), along, (1, 1))
    return [force[k * keep : (k + 1) * keep] for k in range(3)]


def choose(sc, near, fwd):
    lower = sc[S_H] == 0
    return (lambda t: jnp.where(lower, near[0, t], fwd[t])), (lambda t: jnp.where(lower, fwd[t], near[0, t]))


def deposit_kernel(sc, pop, mask, vel, cc, near, fwd, arr, third_in, corner, ends, ye, xb, xa, ccy, hi, lo):
    del corner, ends
    h = sc[S_H]
    lower = h == 0
    up, down = choose(sc, near, fwd)
    for t in range(T_FACE):
        hi[t], lo[t] = up(t), down(t)
    own = particle_fields([arr[2 * s + h] for s in range(16)])
    partner = particle_fields([arr[2 * s + 1 - h] for s in range(16)])
    third = particle_fields([third_in[s // 4, 2 * (s % 4) : 2 * (s % 4) + 2, :] for s in range(16)])
    high = [jnp.where(lower, a, b) for a, b in zip(partner, third)]
    low = [jnp.where(lower, b, a) for a, b in zip(partner, third)]
    rows32 = iota((32, 1), 0)
    force = deposit(
        own,
        [jnp.concatenate([vel[k, x] for x in range(4)], axis=0) for k in range(3)],
        rows32 >> 3,
        rows32 & 7,
        32,
    )
    row = iota((8, 128), 0)
    first_half = row < 4

    def layer(base, k):
        a, b = hi[base + k // 2], lo[base + k // 2]
        return jnp.where(first_half, roll(a, 4, 0), b) if k % 2 else jnp.where(first_half, a, roll(b, 4, 0))

    n1 = [layer(0, ch) for ch in range(27)]
    g1 = layer(0, 27)
    n2 = [layer(T_DEEP, k) for k in range(9)]
    density2, m2, g2 = layer(T_DEEP, 9), [layer(T_DEEP, 10 + k) for k in range(3)], layer(T_DEEP, 13)
    v3 = [layer(T_DEEP, 14 + k) for k in range(3)]
    density1, m1 = moments(n1)
    inverse1, inverse2 = 1.0 / (density1 + (1.0 - g1)), 1.0 / (density2 + (1.0 - g2))
    rows16 = iota((16, 1), 0)
    pushed = []
    for above, fields in ((True, high), (False, low)):
        velocity = []
        for k in range(3):
            a, b = m1[k] * inverse1, m2[k] * inverse2
            c = jnp.where(first_half, v3[k] if above else roll(v3[k], 4, 0), 0.0)
            ab = jnp.where(first_half, a, roll(b, 4, 0)) if above else jnp.where(first_half, roll(a, 4, 0), b)
            velocity.append(jnp.concatenate([ab, c], axis=0))
        depth = rows16 >> 2
        pushed.append(deposit(fields, velocity, rows16 & 3, depth if above else 7 - depth, 8))
    f1 = [jnp.where(first_half, a, roll(b, 4, 0)) for a, b in zip(*pushed)]
    f2 = [jnp.where(first_half, roll(a, 4, 0), b) for a, b in zip(*pushed)]
    side1 = collide(n1, g1, f1, tau_fine) + [g1] + f1
    s2 = density2 + (1.0 - g2)
    u2 = [(m2[k] + tau_fine * f2[k]) * inverse2 for k in range(3)]
    u2[1] = jnp.where(first_half, u2[1], -u2[1])
    e2 = equilibrium(s2 * (1.0 / tau_fine), u2)
    side2 = [
        jnp.where(g2 > 0.0, (1.0 - 1.0 / tau_fine) * n2[k] + e2[DOWN[1][k]], wall) for k in range(9)
    ]
    for x in range(4):
        g = mask[x].astype(jnp.float32)
        f = [force[k][8 * x : 8 * x + 8] for k in range(3)]
        mine = collide([pop[i, x] for i in range(27)], g, f, tau_fine) + [g] + f
        for ch in range(31):
            ye[x, ch, 0:8, :] = mine[ch]
            value = jnp.where(row == 0, roll(side1[ch], -x, 0), 0.0)
            value = jnp.where(row == 7, roll(side1[ch], 3 - x, 0), value)
            if ch in DOWN[1]:
                value = jnp.where(row == 1, roll(side2[DOWN[1].index(ch)], 1 - x, 0), value)
            if ch in UP[1]:
                value = jnp.where(row == 6, roll(side2[UP[1].index(ch)], 2 - x, 0), value)
            ye[x, ch, 8:16, :] = value
    ccy[...] = cc[...]
    has_hi, has_lo = sc[S_YHI] == 1, sc[S_YLO] == 1
    for face, way, has, r in ((hi, DOWN[1], has_hi, 4), (lo, UP[1], has_lo, 7)):
        for j, i in enumerate(way):
            lane = 64 * (j // 5)
            for x in range(8):
                value = face[T_COARSE + j % 5, x : x + 1, lane : lane + 64]
                ccy[x, i, r : r + 1, 0:64] = jnp.where(has, value, wall)
    even = sc[S_CORE] == 0
    outer = (row < 2) | (row >= 6)

    def send(t, a, b):
        xa[t], xb[t] = jnp.where(even, a, b), jnp.where(even, b, a)

    ups = [(3, ch) for ch in range(31)] + [(2, i) for i in UP[0]]
    downs = [(0, ch) for ch in range(31)] + [(1, i) for i in DOWN[0]]
    for k in range(40):
        send(k, ye[ups[k] + (slice(0, 8),)], ye[downs[k] + (slice(0, 8),)])
    for k in range(20):
        pairs = []
        for which in (ups, downs):
            first, second = which[2 * k], which[2 * k + 1]
            value = roll(ye[second + (slice(8, 16),)], 4, 0)
            pairs.append(jnp.where(outer, ye[first + (slice(8, 16),)], value))
        send(X_ROWS + k, *pairs)
    for j in range(9):
        send(X_COARSE + j, ccy[7, UP[0][j]], ccy[0, DOWN[0][j]])


def x_tile(ye, up, down, x, ch):
    if 2 <= x <= 5:
        return ye[x - 2, ch]
    face = down if x < 2 else up
    slot = ch if x in (1, 6) else 31 + (UP[0] if x == 0 else DOWN[0]).index(ch)
    row = iota((8, 128), 0)
    rest = roll(face(X_ROWS + slot // 2), 4 * (slot % 2), 0)
    return jnp.concatenate([face(slot), jnp.where((row < 2) | (row >= 6), rest, 0.0)], axis=0)


def pick(sc, index, a, b):
    even = sc[index] == 0
    return (lambda t: jnp.where(even, a[t], b[t])), (lambda t: jnp.where(even, b[t], a[t]))


def level_layers(sc, rs, inflow, near, fwd, ends, corner, swr, sw, inf):
    wide = T_FACE - T_LEVEL
    for h in range(2):
        here, there, other, beyond = ((3, 2), (0, 1), (4, 5), (7, 6)) if h == 0 else ((0, 1), (3, 2), (7, 6), (4, 5))

        def put(ch, source, base, rows, ref, to):
            for depth in range(2):
                if (ch, depth) in LEVEL:
                    tile, at, lane = LEVEL[ch, depth]
                    r = rows[depth]
                    ref[r : r + 1, to : to + 64] = source[tile + base, at : at + 1, lane : lane + 64]

        def received(channels):
            for q, ch in enumerate(channels):
                ref, to = swr.at[q // 2], 64 * (q % 2)
                put(ch, ends, -T_LEVEL, here, ref, to)
                put(ch, ends, wide - T_LEVEL, there, ref, to)
                put(ch, ends, 2 * wide - T_LEVEL, other, ref, to)
                put(ch, corner, -T_LEVEL, beyond, ref, to)

        @pl.when((sc[S_FIRST] == 1) & (sc[S_H] == h))
        def _():
            received(range(36))
            for j in range(9):
                ref, to = sw.at[j // 2], 64 * (j % 2)
                ref[0:4, to : to + 64] = rs[j, 0:4, 0:64]
                put(36 + j, near.at[0], 0, other, ref, to)
                put(36 + j, fwd, 0, beyond, ref, to)
            inf[0:4, 0:64] = inflow[...]
            put(45, near.at[0], 0, other, inf, 0)
            put(45, fwd, 0, beyond, inf, 0)

        @pl.when((sc[S_LAST] == 1) & (sc[S_H] == h))
        def _():
            received(range(36, 45))


def column_kernel(
    sc, ye, xbr, xar, ccy, rs, inflow, near, fwd, ends, corner, za, zb, swr, sw, inf
):
    level_layers(sc, rs, inflow, near, fwd, ends, corner, swr, sw, inf)
    up, down = pick(sc, S_CORE, xar, xbr)
    lane = iota((16, 128), 1)
    lane8 = iota((8, 128), 1)
    made = {}
    for way in (1, -1):
        tiles = [jnp.zeros((16, 128), jnp.float32) for _ in range(3)]
        for (depth, x, ch), spot in ZL[way].items():
            source = 127 - depth if way > 0 else depth
            value = roll(x_tile(ye, up, down, x, ch), spot - source, 1)
            tiles[spot // 128] = jnp.where(lane == spot % 128, value, tiles[spot // 128])
        out = [t[8 * k : 8 * k + 8] for t in tiles for k in range(2)]
        tiles = [jnp.zeros((8, 128), jnp.float32) for _ in range(2)]
        for item, spot in CL[way].items():
            if item[0] == "c":
                _, x, i = item
                if x == 0:
                    value = down(X_COARSE + UP[0].index(i))
                elif x == 9:
                    value = up(X_COARSE + DOWN[0].index(i))
                else:
                    value = ccy[x - 1, i]
                source = 63 if way > 0 else 0
            elif item[0] == "g":
                _, ch, depth = item
                q = ch if ch < 36 else ch - 36
                value = swr[q // 2] if ch < 36 else sw[q // 2]
                source = (63 - depth if way > 0 else depth) + 64 * (q % 2)
            else:
                value = inf[...]
                source = 63 if way > 0 else 0
            value = roll(value, spot - source, 1)
            tiles[spot // 128] = jnp.where(lane8 == spot % 128, value, tiles[spot // 128])
        made[way] = out + tiles
    even = sc[S_ODD] == 0
    for t in range(8):
        za[t] = jnp.where(even, made[1][t], made[-1][t])
        zb[t] = jnp.where(even, made[-1][t], made[1][t])


def step_kernel(
    sc, ye, xbr, xar, swr, ccy, sw, inf, zar, zbr, fine, coarse, p1, p2, gx, fx, ce, gr, late
):
    up, down = pick(sc, S_CORE, xar, xbr)
    zup, zdown = pick(sc, S_ODD, zar, zbr)
    has_yhi, has_ylo, has_zhi, has_zlo = [sc[k] == 1 for k in (S_YHI, S_YLO, S_ZHI, S_ZLO)]
    first, last = sc[S_FIRST] == 1, sc[S_LAST] == 1
    fz_up = [jnp.concatenate([zup(2 * k), zup(2 * k + 1)], axis=0) for k in range(3)]
    fz_down = [jnp.concatenate([zdown(2 * k), zdown(2 * k + 1)], axis=0) for k in range(3)]
    cz_up, cz_down = [zup(6), zup(7)], [zdown(6), zdown(7)]
    lane = iota((16, 128), 1)
    lane8 = iota((8, 128), 1)

    def side(x, ch):
        blank = wall if ch < 27 else 0.0
        value = jnp.zeros((16, 128), jnp.float32)
        for depth in range(2):
            for way, source, has, at in ((-1, fz_up, has_zhi, depth), (1, fz_down, has_zlo, 127 - depth)):
                spot = ZL[way].get((depth, x, ch))
                if spot is not None:
                    moved = jnp.where(has, roll(source[spot // 128], at - spot, 1), blank)
                    value = jnp.where(lane == at, moved, value)
        return value

    for x in range(8):
        for ch in range(31) if 0 < x < 7 else (UP[0] if x == 0 else DOWN[0]):
            main, rest = x_tile(ye, up, down, x, ch), side(x, ch)
            if ch < 27:
                to = p1.at[x, ch]
            elif ch == 27:
                to = gx.at[x - 1]
            else:
                to = fx.at[x - 1, ch - 28]
            to[:, 0:128] = main
            to[:, 128:256] = rest

    row8 = iota((8, 128), 0)
    inside = (row8 < 4) | ((row8 < 6) & has_yhi) | ((row8 >= 6) & has_ylo)
    inside = inside & (
        (lane8 < 64) | ((lane8 >= 64) & (lane8 < 66) & has_zhi) | ((lane8 >= 126) & has_zlo)
    )

    def c_side(value, up_item, down_item, blank, at=64, end=127):
        for way, source, has, item, to in ((-1, cz_up, has_zhi, up_item, at), (1, cz_down, has_zlo, down_item, end)):
            spot = CL[way].get(item)
            if spot is not None:
                moved = jnp.where(has, roll(source[spot // 128], to - spot, 1), blank)
                value = jnp.where(lane8 == to, moved, value)
        return value

    def ghost(ch, ref, q):
        value = roll(ref[q // 2], 64 * (q % 2), 1)
        value = jnp.where(lane8 < 64, value, 0.0)
        for depth in range(2):
            item = ("g", ch, depth)
            value = c_side(value, item, item, 0.0, 64 + depth, 127 - depth)
        return value

    for x in range(8):
        for i in range(27):
            ce[x + 1, i] = c_side(ccy[x, i], ("c", x + 1, i), ("c", x + 1, i), wall)
    inflow = c_side(inf[...], ("i",), ("i",), 0.0)
    zero = jnp.zeros((8, 128), jnp.float32)
    inlet = equilibrium(jnp.ones((8, 128), jnp.float32), [inflow, zero, zero])
    for j in range(9):
        i = UP[0][j]
        came = c_side(down(X_COARSE + j), ("c", 0, i), ("c", 0, i), wall)
        ce[0, i] = jnp.where(first, jnp.where(inside, inlet[i], wall), came)
        i = DOWN[0][j]
        came = c_side(up(X_COARSE + j), ("c", 9, i), ("c", 9, i), wall)
        ce[9, i] = jnp.where(last, jnp.where(inside, ghost(j, swr, j), wall), came)
    for i in range(27):
        a, b, c = stencil[i]
        for x in range(8):
            value = roll(roll(ce[x + 1 - a, i], b, 0), c, 1)
            value = jnp.where(value > limit, value, ce[x + 1, 26 - i])
            coarse[i, x] = value[0:4, 0:64]

    @pl.when(first)
    def _():
        n127 = [ghost(i, swr, i) for i in range(27)]
        post = collide(n127, None, None, tau_coarse)
        for i in range(27):
            gr[1, i] = jnp.where(inside, post[i], wall)
        for j in range(9):
            gr[0, UP[0][j]] = jnp.where(inside, ghost(27 + j, swr, 27 + j), wall)
            gr[2, DOWN[0][j]] = jnp.where(inside, ghost(36 + j, sw, j), wall)
        later = []
        for i in range(27):
            a, b, c = stencil[i]
            value = roll(roll(gr[1 - a, i], b, 0), c, 1)
            value = jnp.where(value > limit, value, gr[1, 26 - i])
            later.append(jnp.where(inside, 0.5 * (n127[i] + value), 0.0))
        wide = ((iota((128, 256), 1) >> 1) == iota((128, 256), 0)).astype(jnp.float32)
        tall = ((iota((432, 216), 0) >> 1) == iota((432, 216), 1)).astype(jnp.float32)
        row16, lane256 = iota((16, 256), 0), iota((16, 256), 1)
        within = (row16 < 8) | ((row16 < 12) & has_yhi) | ((row16 >= 12) & has_ylo)
        within = within & (
            (lane256 < 128) | ((lane256 < 132) & has_zhi) | ((lane256 >= 252) & has_zlo)
        )
        for layer, to in ((n127, p1.at[1]), (later, late)):
            layer = interface(layer, prolong_factor)
            fines = dot(tall, dot(jnp.concatenate(layer, axis=0), wide))
            for i in range(27):
                to[i] = jnp.where(within, fines[16 * i : 16 * i + 16], wall)

    @pl.when(last)
    def _():
        for i in range(27):
            p1[6, i] = p1[5, i]

    def stream_layer(m, carry):
        g = gx[m]
        for i in range(27):
            a, b, c = stencil[i]
            value = roll(roll(p1[m + 1 - a, i], b, 0), c, 1)
            value = jnp.where(value > limit, value, p1[m + 1, 26 - i])
            p2[m, i] = jnp.where(g > 0.0, value, 0.0)
        return carry

    lax.fori_loop(0, 6, stream_layer, 0)

    def collide_layer(m, carry):
        for y in range(2):
            for z in range(2):
                rows, lanes = slice(8 * y, 8 * y + 8), slice(128 * z, 128 * z + 128)
                post = collide(
                    [p2[m, i, rows, lanes] for i in range(27)],
                    gx[m, rows, lanes],
                    [fx[m, k, rows, lanes] for k in range(3)],
                    tau_fine,
                )
                for i in range(27):
                    p2[m, i, rows, lanes] = post[i]
        return carry

    lax.fori_loop(0, 6, collide_layer, 0)

    @pl.when(first)
    def _():
        for i in range(27):
            p2[0, i] = late[i]

    @pl.when(last)
    def _():
        for i in range(27):
            p2[5, i] = p2[4, i]

    def finish_layer(x, carry):
        g = gx[x + 1, 0:8, 0:128]
        for i in range(27):
            a, b, c = stencil[i]
            value = roll(roll(p2[x + 1 - a, i], b, 0), c, 1)[0:8, 0:128]
            value = jnp.where(value > limit, value, p2[x + 1, 26 - i, 0:8, 0:128])
            fine[i, x] = jnp.where(g > 0.0, value, 0.0)
        return carry

    lax.fori_loop(0, 4, finish_layer, 0)


def f32(*shape):
    return jax.ShapeDtypeStruct(shape, jnp.float32)


def call(kernel, name, out_shape, scratch, *args, held=0, cost=0):
    vmem = pl.BlockSpec(memory_space=pltpu.VMEM)
    raw = pl.BlockSpec(memory_space=pltpu.HBM)
    return pl.pallas_call(
        kernel,
        out_shape=out_shape,
        in_specs=[pl.BlockSpec(memory_space=pltpu.SMEM)] + [raw] * held + [vmem] * (len(args) - 1 - held),
        out_specs=[vmem] * len(out_shape),
        scratch_shapes=[pltpu.VMEM(s, jnp.float32) for s in scratch]
        + ([pltpu.SemaphoreType.DMA((held,))] if held else []),
        compiler_params=pltpu.CompilerParams(vmem_limit_bytes=40 * 1024 * 1024),
        cost_estimate=pl.CostEstimate(flops=cost, bytes_accessed=1, transcendentals=0) if cost else None,
        name=name,
    )(*args)


def body(pop, cpop, mask, inflow, part_dest, part_cell, part_vel, part_frac, part_drag):
    gx, gy, h, gz = [lax.axis_index(a) for a in ("gx", "y", "h", "gz")]
    n_gx, n_y, n_gz = lax.axis_size("gx"), lax.axis_size("y"), lax.axis_size("gz")
    row = gy * 2 + h
    sc = jnp.stack(
        [
            h,
            gx % 2,
            gz % 2,
            (gx == 0).astype(jnp.int32),
            (gx == n_gx - 1).astype(jnp.int32),
            (row > 0).astype(jnp.int32),
            (row < 2 * n_y - 1).astype(jnp.int32),
            (gz > 0).astype(jnp.int32),
            (gz < n_gz - 1).astype(jnp.int32),
        ]
    ).astype(jnp.int32)
    faces, vel, cc, r127, rs = call(
        pack_kernel,
        "pack",
        [
            f32(2, T_FACE, 8, 128),
            f32(3, 4, 8, 128),
            f32(8, 27, 8, 128),
            f32(27, 8, 128),
            f32(9, 8, 128),
        ],
        [(27, 8, 8, 128), (4, 4, 8, 128)],
        sc,
        pop,
        cpop,
        mask,
        inflow,
    )
    (outbox,) = call(
        route_kernel,
        "route",
        [f32(64, 128)],
        [],
        sc,
        part_dest.reshape(1, 256),
        part_cell.reshape(1, 256),
        part_vel,
        part_frac,
        part_drag.reshape(1, 256),
        rs,
        cost=50_000_000_000,
    )
    last = n_gx - 1
    spot = lambda x, y, z: (x * n_y + y) * 2 + z
    far_ends = [(spot(a, y, 1), spot(b, y + 1, 0)) for a, b in ((0, last), (last, 0)) for y in range(n_y - 1)]
    corner = lax.ppermute(
        faces[1, T_LEVEL:T_FACE], ("gx", "y", "h"), far_ends + [(j, i) for i, j in far_ends]
    )
    near = lax.ppermute(faces, "h", [(0, 1), (1, 0)])
    arr = lax.all_to_all(outbox.reshape(2 * n_gx, 2, 128), ("gx", "h"), 0, 0, tiled=True)
    near_ends = [(2 * last + 1, 0), (2 * last, 1)]
    ends = lax.ppermute(
        jnp.concatenate(
            [near[0, T_LEVEL:T_FACE], near[1, T_LEVEL:T_FACE], faces[0, T_LEVEL:T_FACE]], axis=0
        ),
        ("gx", "h"),
        near_ends + [(j, i) for i, j in near_ends],
    )
    onward = [(2 * y, 2 * y + 2) for y in range(n_y - 1)]
    onward += [(2 * y + 3, 2 * y + 1) for y in range(n_y - 1)]
    partner = jnp.where(h == 0, arr[1::2], arr[0::2]).reshape(4, 8, 128)
    fwd = lax.ppermute(near[1], ("y", "h"), onward)
    partner, _ = lax.optimization_barrier((partner, near))
    third = lax.ppermute(partner, ("y", "h"), onward)
    ye, xb, xa, ccy = call(
        deposit_kernel,
        "deposit",
        [f32(4, 31, 16, 128), f32(T_X, 8, 128), f32(T_X, 8, 128), f32(8, 27, 8, 128)],
        [(T_FACE, 8, 128), (T_FACE, 8, 128)],
        sc,
        pop,
        mask,
        vel,
        cc,
        near,
        fwd,
        arr,
        third,
        corner,
        ends,
        cost=50_000_000_000,
    )
    inner = [(i, i + 1) for i in range(1, n_gx - 1, 2)]
    xbr = lax.ppermute(xb, "gx", inner + [(j, i) for i, j in inner])
    xar = lax.ppermute(xa, "gx", [(i, i ^ 1) for i in range(n_gx)])
    za, zb, swr, sw, inf = call(
        column_kernel,
        "columns",
        [f32(8, 8, 128), f32(8, 8, 128), f32(T_SW, 8, 128), f32(5, 8, 128), f32(8, 128)],
        [],
        sc,
        ye,
        xbr,
        xar,
        ccy,
        rs,
        inflow,
        near,
        fwd,
        ends,
        corner,
    )
    zar = lax.ppermute(za, "gz", [(i, i ^ 1) for i in range(n_gz)])
    inner = [(i, i + 1) for i in range(1, n_gz - 1, 2)]
    zbr = lax.ppermute(zb, "gz", inner + [(j, i) for i, j in inner])
    fine, coarse = call(
        step_kernel,
        "steps",
        [f32(27, 4, 8, 128), f32(27, 8, 4, 64)],
        [
            (8, 27, 16, 256),
            (6, 27, 16, 256),
            (6, 16, 256),
            (6, 3, 16, 256),
            (10, 27, 8, 128),
            (3, 27, 8, 128),
            (27, 16, 256),
        ],
        sc,
        ye,
        xbr,
        xar,
        swr,
        ccy,
        sw,
        inf,
        zar,
        zbr,
    )
    return fine, coarse


def solution(mesh):
    n_gx, n_gy, n_gz = [mesh.shape[a] for a in ("gx", "gy", "gz")]
    split = Mesh(mesh.devices.reshape(n_gx, n_gy // 2, 2, n_gz), ("gx", "y", "h", "gz"))
    gy = ("y", "h")
    return jax.shard_map(
        body,
        mesh=split,
        in_specs=(
            P(None, "gx", gy, "gz"),
            P(None, "gx", gy, "gz"),
            P("gx", gy, "gz"),
            P(gy, "gz"),
            P("gx", gy, "gz", None, None),
            P("gx", gy, "gz", None),
            P("gx", gy, "gz", None, None),
            P("gx", gy, "gz", None, None),
            P("gx", gy, "gz", None),
        ),
        out_specs=(P(None, "gx", gy, "gz"), P(None, "gx", gy, "gz")),
        check_vma=False,
    )
```

```python
import jax
import jax.numpy as jnp
from jax import lax
from jax.experimental import pallas as pl
from jax.experimental.pallas import tpu as pltpu
from jax.sharding import Mesh, PartitionSpec as P

tau_fine = 1.3
tau_coarse = 0.9
prolong_factor = (tau_fine - 1.0) / (2.0 * tau_coarse)
restrict_factor = 2.0 * (tau_coarse - 1.0) / tau_fine
stencil = [(a, b, c) for a in (-1, 0, 1) for b in (-1, 0, 1) for c in (-1, 0, 1)]
class_weight = (8.0 / 27.0, 2.0 / 27.0, 1.0 / 54.0, 1.0 / 216.0)
wall = -1e30
limit = -1e29


def moving(axis, way):
    return [i for i in range(27) if stencil[i][axis] == way]


UP = [moving(axis, 1) for axis in range(3)]
DOWN = [moving(axis, -1) for axis in range(3)]

T_DEEP, T_COARSE, T_LEVEL, T_FACE = 14, 23, 22, 33
X_ROWS, X_COARSE, T_X = 40, 60, 69


def level_rows():
    rows = [(ch, 0) for ch in range(46)] + [(ch, 1) for ch in range(45)]
    spots = [(22, r, 64 * half) for r in range(4, 8) for half in range(2)]
    spots += [(27, r, 64) for r in range(8)]
    spots += [(t, r, 64 * half) for t in range(28, 33) for r in range(8) for half in range(2)]
    return dict(zip(rows, spots))


LEVEL = level_rows()
T_SW = 18

z_items = [(0, x, ch) for x in range(1, 7) for ch in range(31)]
z_items += [(0, 0, i) for i in UP[0]] + [(0, 7, i) for i in DOWN[0]]
z_deep = [(1, x, j) for x in range(1, 7) for j in range(9)]


def z_layout(way):
    inward = UP[2] if way > 0 else DOWN[2]
    items = list(z_items) + [(1, x, inward[j]) for (_, x, j) in z_deep]
    items += [(1, 0, i) for i in inward if stencil[i][0] == 1]
    items += [(1, 7, i) for i in inward if stencil[i][0] == -1]
    return {item: spot for spot, item in enumerate(items)}


def c_layout(way):
    inward = UP[2] if way > 0 else DOWN[2]
    items = [("c", x, i) for x in range(1, 9) for i in inward]
    items += [("c", 0, i) for i in inward if stencil[i][0] == 1]
    items += [("c", 9, i) for i in inward if stencil[i][0] == -1]
    items += [("g", ch, 0) for ch in range(45)] + [("g", ch, 1) for ch in range(27)]
    items += [("g", 27 + j, 1) for j in range(9) if stencil[UP[0][j]][2] == way]
    items += [("g", 36 + j, 1) for j in range(9) if stencil[DOWN[0][j]][2] == way]
    items += [("i",)]
    return {item: spot for spot, item in enumerate(items)}


ZL = {1: z_layout(1), -1: z_layout(-1)}
CL = {1: c_layout(1), -1: c_layout(-1)}


def roll(value, by, axis):
    by = by % value.shape[axis]
    return value if by == 0 else pltpu.roll(value, by, axis)


def iota(shape, axis):
    return lax.broadcasted_iota(jnp.int32, shape, axis)


def dot(a, b, contract=(1, 0)):
    return lax.dot_general(
        a,
        b,
        (((contract[0],), (contract[1],)), ((), ())),
        precision=lax.Precision.HIGHEST,
        preferred_element_type=jnp.float32,
    )


def select(value, pick, left=False):
    total = None
    pick = pick.astype(jnp.bfloat16)
    for _ in range(3):
        part = value.astype(jnp.bfloat16)
        value = value - part.astype(jnp.float32)
        a, b = (pick, part) if left else (part, pick)
        product = jnp.dot(a, b, preferred_element_type=jnp.float32)
        total = product if total is None else total + product
    return total


def moments(n):
    totals = [n[13], None, None, None]
    parts = [[None] * 4 for _ in range(3)]
    for i in range(14, 27):
        c = stencil[i]
        k = abs(c[0]) + abs(c[1]) + abs(c[2])
        both, odd = n[i] + n[26 - i], n[i] - n[26 - i]
        totals[k] = both if totals[k] is None else totals[k] + both
        for axis in range(3):
            if c[axis]:
                have = parts[axis][k]
                if have is None:
                    parts[axis][k] = odd if c[axis] > 0 else -odd
                else:
                    parts[axis][k] = have + odd if c[axis] > 0 else have - odd
    density = sum(class_weight[k] * totals[k] for k in range(4))
    momentum = [sum(class_weight[k] * parts[axis][k] for k in (1, 2, 3)) for axis in range(3)]
    return density, momentum


def equilibrium(s, u):
    base = s - (1.5 * (u[0] * u[0] + u[1] * u[1] + u[2] * u[2])) * s
    s3, s45 = 3.0 * s, 4.5 * s
    out = [None] * 27
    out[13] = base
    for i in range(14, 27):
        cu = None
        for axis in range(3):
            c = stencil[i][axis]
            if c:
                if cu is None:
                    cu = u[axis] if c > 0 else -u[axis]
                else:
                    cu = cu + u[axis] if c > 0 else cu - u[axis]
        even, odd = base + s45 * (cu * cu), s3 * cu
        out[i], out[26 - i] = even + odd, even - odd
    return out


def collide(n, g, force, tau):
    density, m = moments(n)
    s = jnp.where(density == 0.0, 1.0, density) if g is None else density + (1.0 - g)
    inverse = 1.0 / s
    if force is not None:
        m = [m[k] + tau * force[k] for k in range(3)]
    e = equilibrium(s * (1.0 / tau), [v * inverse for v in m])
    post = [(1.0 - 1.0 / tau) * n[i] + e[i] for i in range(27)]
    return post if g is None else [jnp.where(g > 0.0, p, wall) for p in post]


def interface(n, factor):
    density, m = moments(n)
    density = jnp.where(density == 0.0, 1.0, density)
    inverse = 1.0 / density
    e = equilibrium(density, [v * inverse for v in m])
    return [e[i] + factor * (n[i] - e[i]) for i in range(27)]


S_H, S_CORE, S_ODD, S_FIRST, S_LAST, S_YLO, S_YHI, S_ZLO, S_ZHI = range(9)


def route_kernel(sc, pdest, pcell, pvel, pfrac, pdrag, anchor, outbox):
    del sc, anchor
    dest = pdest[...]
    onehot = (iota((16, 256), 0) == dest).astype(jnp.float32)
    earlier = (iota((256, 256), 0) < iota((256, 256), 1)).astype(jnp.bfloat16)
    before = jnp.dot(onehot.astype(jnp.bfloat16), earlier, preferred_element_type=jnp.float32)
    rank = jnp.sum(onehot * before, axis=0, keepdims=True).astype(jnp.int32)
    slot = (iota((32, 256), 0) == rank).astype(jnp.float32)
    row = iota((64, 256), 0)
    hit = (row >> 2) == dest
    odd = (row & 1) == 1
    fields = [pvel[0, 0, 0, k : k + 1, :] for k in range(3)] + [pdrag[...]]
    fields += [pfrac[0, 0, 0, k : k + 1, :] for k in range(3)] + [pcell[...].astype(jnp.float32)]
    for q in range(4):
        values = jnp.where(hit, jnp.where(odd, fields[4 + q], fields[q]), 0.0)
        outbox[:, 32 * q : 32 * q + 32] = dot(values, slot, (1, 1))


def pack_kernel(
    sc, pop, cpop, mask, inflow, faces, vel, cc, r127, rs, rc, mom,
):
    h = sc[S_H]
    rc[...] = jnp.zeros(rc.shape, jnp.float32)
    faces[...] = jnp.zeros(faces.shape, jnp.float32)
    for x in range(4):
        density, m = moments([pop[i, x] for i in range(27)])
        inverse = 1.0 / (density + (1.0 - mask[x].astype(jnp.float32)))
        mom[0, x] = density
        for k in range(3):
            mom[k + 1, x] = m[k]
            vel[k, x] = m[k] * inverse
    for i in range(27):
        rc[i, :, 0:4, 0:64] = cpop[i]
        r127[i] = rc[i, 7]
    for x in range(8):
        post = collide([rc[i, x] for i in range(27)], None, None, tau_coarse)
        for i in range(27):
            cc[x, i] = post[i]
    pair = jnp.concatenate([pop[i, 0] + pop[i, 1] for i in range(27)], axis=0)
    narrow = ((iota((128, 128), 0) >> 1) == iota((128, 128), 1)).astype(jnp.float32)
    down, across = iota((216, 216), 0), iota((216, 216), 1)
    low = ((down >> 3) == (across >> 3)) & (((across & 7) >> 1) == (down & 7))
    mean = 0.125 * select(select(pair, narrow), low.astype(jnp.float32), left=True)
    settled = interface([mean[8 * i : 8 * i + 8] for i in range(27)], restrict_factor)
    for j in range(9):
        rs[j] = settled[DOWN[0][j]]
    for way in (1, -1):
        face = h if way > 0 else 1 - h
        depths, coarse_depths = ((7, 6, 5), (3, 2)) if way > 0 else ((0, 1, 2), (0, 1))
        inward = UP[1] if way > 0 else DOWN[1]
        for x in range(4):

            def put(base, k, ref, depth):
                at = 4 * (k % 2) + x
                value = ref[depth : depth + 1, :].astype(jnp.float32)
                faces[face, base + k // 2, at : at + 1, :] = value

            for ch in range(27):
                put(0, ch, pop.at[ch, x], depths[0])
            put(0, 27, mask.at[x], depths[0])
            for k in range(9):
                put(T_DEEP, k, pop.at[inward[k], x], depths[1])
            for k in range(4):
                put(T_DEEP, 9 + k, mom.at[k, x], depths[1])
            put(T_DEEP, 13, mask.at[x], depths[1])
            for k in range(3):
                put(T_DEEP, 14 + k, vel.at[k, x], depths[2])
        r = coarse_depths[0]
        for j, i in enumerate(inward):
            lane = 64 * (j // 5)
            for x in range(8):
                faces[face, T_COARSE + j % 5, x : x + 1, lane : lane + 64] = cc[x, i, r : r + 1, 0:64]
        for (ch, depth), (tile, at, lane) in LEVEL.items():
            r = coarse_depths[depth]
            if ch < 27:
                value = rc[ch, 7, r : r + 1, 0:64]
            elif ch < 36:
                value = cc[6, UP[0][ch - 27], r : r + 1, 0:64]
            elif ch < 45:
                value = rs[ch - 36, r : r + 1, 0:64]
            else:
                value = inflow[r : r + 1, :]
            faces[face, tile, at : at + 1, lane : lane + 64] = value


def particle_fields(rows):
    lane = iota((2, 128), 1) >> 5
    chunks = [[] for _ in range(4)]
    for k in range(4):
        turned = [[roll(rows[4 * k + j], 32 * s, 1) for s in range(4)] for j in range(4)]
        for q in range(4):
            value = turned[0][(0 - q) % 4]
            for j in range(1, 4):
                value = jnp.where(lane == j, turned[j][(j - q) % 4], value)
            chunks[q].append(value)
    flat = [jnp.concatenate(chunks[q], axis=1) for q in range(4)]
    return [flat[f % 4][f // 4 : f // 4 + 1, :] for f in range(8)]


def deposit(fields, velocity, xr, yr, keep):
    rows = velocity[0].shape[0]
    count = fields[0].shape[1]
    cell = fields[7].astype(jnp.int32)
    ix, iy, iz = cell >> 10, (cell >> 7) & 7, cell & 127
    fx, fy, fz = fields[4:7]
    lane = iota((128, count), 0)
    along = jnp.where(lane == iz, 1.0 - fz, jnp.where(lane == iz + 1, fz, 0.0))
    across = jnp.where(xr == ix, 1.0 - fx, jnp.where(xr == ix + 1, fx, 0.0))
    across = across * jnp.where(yr == iy, 1.0 - fy, jnp.where(yr == iy + 1, fy, 0.0))
    seen = dot(jnp.concatenate(velocity, axis=0), along)
    pushes = []
    for k in range(3):
        sampled = jnp.sum(seen[k * rows : (k + 1) * rows] * across, axis=0, keepdims=True)
        impulse = fields[3] * (fields[k] - sampled)
        pushes.append(impulse * across[0:keep])
    force = dot(jnp.concatenate(pushes, axis=0), along, (1, 1))
    return [force[k * keep : (k + 1) * keep] for k in range(3)]


def choose(sc, near, fwd):
    lower = sc[S_H] == 0
    return (lambda t: jnp.where(lower, near[0, t], fwd[t])), (lambda t: jnp.where(lower, fwd[t], near[0, t]))


def deposit_kernel(sc, pop, mask, vel, cc, near, fwd, arr, third_in, corner, ends, ye, xb, xa, ccy, hi, lo):
    del corner, ends
    h = sc[S_H]
    lower = h == 0
    up, down = choose(sc, near, fwd)
    for t in range(T_FACE):
        hi[t], lo[t] = up(t), down(t)
    own = particle_fields([arr[2 * s + h] for s in range(16)])
    partner = particle_fields([arr[2 * s + 1 - h] for s in range(16)])
    third = particle_fields([third_in[s // 4, 2 * (s % 4) : 2 * (s % 4) + 2, :] for s in range(16)])
    high = [jnp.where(lower, a, b) for a, b in zip(partner, third)]
    low = [jnp.where(lower, b, a) for a, b in zip(partner, third)]
    rows32 = iota((32, 1), 0)
    force = deposit(
        own,
        [jnp.concatenate([vel[k, x] for x in range(4)], axis=0) for k in range(3)],
        rows32 >> 3,
        rows32 & 7,
        32,
    )
    row = iota((8, 128), 0)
    first_half = row < 4

    def layer(base, k):
        a, b = hi[base + k // 2], lo[base + k // 2]
        return jnp.where(first_half, roll(a, 4, 0), b) if k % 2 else jnp.where(first_half, a, roll(b, 4, 0))

    n1 = [layer(0, ch) for ch in range(27)]
    g1 = layer(0, 27)
    n2 = [layer(T_DEEP, k) for k in range(9)]
    density2, m2, g2 = layer(T_DEEP, 9), [layer(T_DEEP, 10 + k) for k in range(3)], layer(T_DEEP, 13)
    v3 = [layer(T_DEEP, 14 + k) for k in range(3)]
    density1, m1 = moments(n1)
    inverse1, inverse2 = 1.0 / (density1 + (1.0 - g1)), 1.0 / (density2 + (1.0 - g2))
    rows16 = iota((16, 1), 0)
    pushed = []
    for above, fields in ((True, high), (False, low)):
        velocity = []
        for k in range(3):
            a, b = m1[k] * inverse1, m2[k] * inverse2
            c = jnp.where(first_half, v3[k] if above else roll(v3[k], 4, 0), 0.0)
            ab = jnp.where(first_half, a, roll(b, 4, 0)) if above else jnp.where(first_half, roll(a, 4, 0), b)
            velocity.append(jnp.concatenate([ab, c], axis=0))
        depth = rows16 >> 2
        pushed.append(deposit(fields, velocity, rows16 & 3, depth if above else 7 - depth, 8))
    f1 = [jnp.where(first_half, a, roll(b, 4, 0)) for a, b in zip(*pushed)]
    f2 = [jnp.where(first_half, roll(a, 4, 0), b) for a, b in zip(*pushed)]
    side1 = collide(n1, g1, f1, tau_fine) + [g1] + f1
    s2 = density2 + (1.0 - g2)
    u2 = [(m2[k] + tau_fine * f2[k]) * inverse2 for k in range(3)]
    u2[1] = jnp.where(first_half, u2[1], -u2[1])
    e2 = equilibrium(s2 * (1.0 / tau_fine), u2)
    side2 = [
        jnp.where(g2 > 0.0, (1.0 - 1.0 / tau_fine) * n2[k] + e2[DOWN[1][k]], wall) for k in range(9)
    ]
    for x in range(4):
        g = mask[x].astype(jnp.float32)
        f = [force[k][8 * x : 8 * x + 8] for k in range(3)]
        mine = collide([pop[i, x] for i in range(27)], g, f, tau_fine) + [g] + f
        for ch in range(31):
            ye[x, ch, 0:8, :] = mine[ch]
            value = jnp.where(row == 0, roll(side1[ch], -x, 0), 0.0)
            value = jnp.where(row == 7, roll(side1[ch], 3 - x, 0), value)
            if ch in DOWN[1]:
                value = jnp.where(row == 1, roll(side2[DOWN[1].index(ch)], 1 - x, 0), value)
            if ch in UP[1]:
                value = jnp.where(row == 6, roll(side2[UP[1].index(ch)], 2 - x, 0), value)
            ye[x, ch, 8:16, :] = value
    ccy[...] = cc[...]
    has_hi, has_lo = sc[S_YHI] == 1, sc[S_YLO] == 1
    for face, way, has, r in ((hi, DOWN[1], has_hi, 4), (lo, UP[1], has_lo, 7)):
        for j, i in enumerate(way):
            lane = 64 * (j // 5)
            for x in range(8):
                value = face[T_COARSE + j % 5, x : x + 1, lane : lane + 64]
                ccy[x, i, r : r + 1, 0:64] = jnp.where(has, value, wall)
    even = sc[S_CORE] == 0
    outer = (row < 2) | (row >= 6)

    def send(t, a, b):
        xa[t], xb[t] = jnp.where(even, a, b), jnp.where(even, b, a)

    ups = [(3, ch) for ch in range(31)] + [(2, i) for i in UP[0]]
    downs = [(0, ch) for ch in range(31)] + [(1, i) for i in DOWN[0]]
    for k in range(40):
        send(k, ye[ups[k] + (slice(0, 8),)], ye[downs[k] + (slice(0, 8),)])
    for k in range(20):
        pairs = []
        for which in (ups, downs):
            first, second = which[2 * k], which[2 * k + 1]
            value = roll(ye[second + (slice(8, 16),)], 4, 0)
            pairs.append(jnp.where(outer, ye[first + (slice(8, 16),)], value))
        send(X_ROWS + k, *pairs)
    for j in range(9):
        send(X_COARSE + j, ccy[7, UP[0][j]], ccy[0, DOWN[0][j]])


def x_tile(ye, up, down, x, ch):
    if 2 <= x <= 5:
        return ye[x - 2, ch]
    face = down if x < 2 else up
    slot = ch if x in (1, 6) else 31 + (UP[0] if x == 0 else DOWN[0]).index(ch)
    row = iota((8, 128), 0)
    rest = roll(face(X_ROWS + slot // 2), 4 * (slot % 2), 0)
    return jnp.concatenate([face(slot), jnp.where((row < 2) | (row >= 6), rest, 0.0)], axis=0)


def pick(sc, index, a, b):
    even = sc[index] == 0
    return (lambda t: jnp.where(even, a[t], b[t])), (lambda t: jnp.where(even, b[t], a[t]))


def level_layers(sc, rs, inflow, near, fwd, ends, corner, swr, sw, inf):
    wide = T_FACE - T_LEVEL
    for h in range(2):
        here, there, other, beyond = ((3, 2), (0, 1), (4, 5), (7, 6)) if h == 0 else ((0, 1), (3, 2), (7, 6), (4, 5))

        def put(ch, source, base, rows, ref, to):
            for depth in range(2):
                if (ch, depth) in LEVEL:
                    tile, at, lane = LEVEL[ch, depth]
                    r = rows[depth]
                    ref[r : r + 1, to : to + 64] = source[tile + base, at : at + 1, lane : lane + 64]

        def received(channels):
            for q, ch in enumerate(channels):
                ref, to = swr.at[q // 2], 64 * (q % 2)
                put(ch, ends, -T_LEVEL, here, ref, to)
                put(ch, ends, wide - T_LEVEL, there, ref, to)
                put(ch, ends, 2 * wide - T_LEVEL, other, ref, to)
                put(ch, corner, -T_LEVEL, beyond, ref, to)

        @pl.when((sc[S_FIRST] == 1) & (sc[S_H] == h))
        def _():
            received(range(36))
            for j in range(9):
                ref, to = sw.at[j // 2], 64 * (j % 2)
                ref[0:4, to : to + 64] = rs[j, 0:4, 0:64]
                put(36 + j, near.at[0], 0, other, ref, to)
                put(36 + j, fwd, 0, beyond, ref, to)
            inf[0:4, 0:64] = inflow[...]
            put(45, near.at[0], 0, other, inf, 0)
            put(45, fwd, 0, beyond, inf, 0)

        @pl.when((sc[S_LAST] == 1) & (sc[S_H] == h))
        def _():
            received(range(36, 45))


def column_kernel(
    sc, ye, xbr, xar, ccy, rs, inflow, near, fwd, ends, corner, za, zb, swr, sw, inf
):
    level_layers(sc, rs, inflow, near, fwd, ends, corner, swr, sw, inf)
    up, down = pick(sc, S_CORE, xar, xbr)
    lane = iota((16, 128), 1)
    lane8 = iota((8, 128), 1)
    made = {}
    for way in (1, -1):
        tiles = [jnp.zeros((16, 128), jnp.float32) for _ in range(3)]
        for (depth, x, ch), spot in ZL[way].items():
            source = 127 - depth if way > 0 else depth
            value = roll(x_tile(ye, up, down, x, ch), spot - source, 1)
            tiles[spot // 128] = jnp.where(lane == spot % 128, value, tiles[spot // 128])
        out = [t[8 * k : 8 * k + 8] for t in tiles for k in range(2)]
        tiles = [jnp.zeros((8, 128), jnp.float32) for _ in range(2)]
        for item, spot in CL[way].items():
            if item[0] == "c":
                _, x, i = item
                if x == 0:
                    value = down(X_COARSE + UP[0].index(i))
                elif x == 9:
                    value = up(X_COARSE + DOWN[0].index(i))
                else:
                    value = ccy[x - 1, i]
                source = 63 if way > 0 else 0
            elif item[0] == "g":
                _, ch, depth = item
                q = ch if ch < 36 else ch - 36
                value = swr[q // 2] if ch < 36 else sw[q // 2]
                source = (63 - depth if way > 0 else depth) + 64 * (q % 2)
            else:
                value = inf[...]
                source = 63 if way > 0 else 0
            value = roll(value, spot - source, 1)
            tiles[spot // 128] = jnp.where(lane8 == spot % 128, value, tiles[spot // 128])
        made[way] = out + tiles
    even = sc[S_ODD] == 0
    for t in range(8):
        za[t] = jnp.where(even, made[1][t], made[-1][t])
        zb[t] = jnp.where(even, made[-1][t], made[1][t])


def step_kernel(
    sc, ye, xbr, xar, swr, ccy, sw, inf, zar, zbr, fine, coarse, p1, p2, gx, fx, ce, gr, late
):
    up, down = pick(sc, S_CORE, xar, xbr)
    zup, zdown = pick(sc, S_ODD, zar, zbr)
    has_yhi, has_ylo, has_zhi, has_zlo = [sc[k] == 1 for k in (S_YHI, S_YLO, S_ZHI, S_ZLO)]
    first, last = sc[S_FIRST] == 1, sc[S_LAST] == 1
    fz_up = [jnp.concatenate([zup(2 * k), zup(2 * k + 1)], axis=0) for k in range(3)]
    fz_down = [jnp.concatenate([zdown(2 * k), zdown(2 * k + 1)], axis=0) for k in range(3)]
    cz_up, cz_down = [zup(6), zup(7)], [zdown(6), zdown(7)]
    lane = iota((16, 128), 1)
    lane8 = iota((8, 128), 1)

    def side(x, ch):
        blank = wall if ch < 27 else 0.0
        value = jnp.zeros((16, 128), jnp.float32)
        for depth in range(2):
            for way, source, has, at in ((-1, fz_up, has_zhi, depth), (1, fz_down, has_zlo, 127 - depth)):
                spot = ZL[way].get((depth, x, ch))
                if spot is not None:
                    moved = jnp.where(has, roll(source[spot // 128], at - spot, 1), blank)
                    value = jnp.where(lane == at, moved, value)
        return value

    for x in range(8):
        for ch in range(31) if 0 < x < 7 else (UP[0] if x == 0 else DOWN[0]):
            main, rest = x_tile(ye, up, down, x, ch), side(x, ch)
            if ch < 27:
                to = p1.at[x, ch]
            elif ch == 27:
                to = gx.at[x - 1]
            else:
                to = fx.at[x - 1, ch - 28]
            to[:, 0:128] = main
            to[:, 128:256] = rest

    row8 = iota((8, 128), 0)
    inside = (row8 < 4) | ((row8 < 6) & has_yhi) | ((row8 >= 6) & has_ylo)
    inside = inside & (
        (lane8 < 64) | ((lane8 >= 64) & (lane8 < 66) & has_zhi) | ((lane8 >= 126) & has_zlo)
    )

    def c_side(value, up_item, down_item, blank, at=64, end=127):
        for way, source, has, item, to in ((-1, cz_up, has_zhi, up_item, at), (1, cz_down, has_zlo, down_item, end)):
            spot = CL[way].get(item)
            if spot is not None:
                moved = jnp.where(has, roll(source[spot // 128], to - spot, 1), blank)
                value = jnp.where(lane8 == to, moved, value)
        return value

    def ghost(ch, ref, q):
        value = roll(ref[q // 2], 64 * (q % 2), 1)
        value = jnp.where(lane8 < 64, value, 0.0)
        for depth in range(2):
            item = ("g", ch, depth)
            value = c_side(value, item, item, 0.0, 64 + depth, 127 - depth)
        return value

    for x in range(8):
        for i in range(27):
            ce[x + 1, i] = c_side(ccy[x, i], ("c", x + 1, i), ("c", x + 1, i), wall)
    inflow = c_side(inf[...], ("i",), ("i",), 0.0)
    zero = jnp.zeros((8, 128), jnp.float32)
    inlet = equilibrium(jnp.ones((8, 128), jnp.float32), [inflow, zero, zero])
    for j in range(9):
        i = UP[0][j]
        came = c_side(down(X_COARSE + j), ("c", 0, i), ("c", 0, i), wall)
        ce[0, i] = jnp.where(first, jnp.where(inside, inlet[i], wall), came)
        i = DOWN[0][j]
        came = c_side(up(X_COARSE + j), ("c", 9, i), ("c", 9, i), wall)
        ce[9, i] = jnp.where(last, jnp.where(inside, ghost(j, swr, j), wall), came)
    for i in range(27):
        a, b, c = stencil[i]
        for x in range(8):
            value = roll(roll(ce[x + 1 - a, i], b, 0), c, 1)
            value = jnp.where(value > limit, value, ce[x + 1, 26 - i])
            coarse[i, x] = value[0:4, 0:64]

    @pl.when(first)
    def _():
        n127 = [ghost(i, swr, i) for i in range(27)]
        post = collide(n127, None, None, tau_coarse)
        for i in range(27):
            gr[1, i] = jnp.where(inside, post[i], wall)
        for j in range(9):
            gr[0, UP[0][j]] = jnp.where(inside, ghost(27 + j, swr, 27 + j), wall)
            gr[2, DOWN[0][j]] = jnp.where(inside, ghost(36 + j, sw, j), wall)
        later = []
        for i in range(27):
            a, b, c = stencil[i]
            value = roll(roll(gr[1 - a, i], b, 0), c, 1)
            value = jnp.where(value > limit, value, gr[1, 26 - i])
            later.append(jnp.where(inside, 0.5 * (n127[i] + value), 0.0))
        wide = ((iota((128, 256), 1) >> 1) == iota((128, 256), 0)).astype(jnp.float32)
        tall = ((iota((432, 216), 0) >> 1) == iota((432, 216), 1)).astype(jnp.float32)
        row16, lane256 = iota((16, 256), 0), iota((16, 256), 1)
        within = (row16 < 8) | ((row16 < 12) & has_yhi) | ((row16 >= 12) & has_ylo)
        within = within & (
            (lane256 < 128) | ((lane256 < 132) & has_zhi) | ((lane256 >= 252) & has_zlo)
        )
        for layer, to in ((n127, p1.at[1]), (later, late)):
            layer = interface(layer, prolong_factor)
            fines = select(select(jnp.concatenate(layer, axis=0), wide), tall, left=True)
            for i in range(27):
                to[i] = jnp.where(within, fines[16 * i : 16 * i + 16], wall)

    @pl.when(last)
    def _():
        for i in range(27):
            p1[6, i] = p1[5, i]

    def stream_layer(m, carry):
        g = gx[m]
        for i in range(27):
            a, b, c = stencil[i]
            value = roll(roll(p1[m + 1 - a, i], b, 0), c, 1)
            value = jnp.where(value > limit, value, p1[m + 1, 26 - i])
            p2[m, i] = jnp.where(g > 0.0, value, 0.0)
        return carry

    lax.fori_loop(0, 6, stream_layer, 0)

    def collide_layer(m, carry):
        for y in range(2):
            for z in range(2):
                rows, lanes = slice(8 * y, 8 * y + 8), slice(128 * z, 128 * z + 128)
                post = collide(
                    [p2[m, i, rows, lanes] for i in range(27)],
                    gx[m, rows, lanes],
                    [fx[m, k, rows, lanes] for k in range(3)],
                    tau_fine,
                )
                for i in range(27):
                    p2[m, i, rows, lanes] = post[i]
        return carry

    lax.fori_loop(0, 6, collide_layer, 0)

    @pl.when(first)
    def _():
        for i in range(27):
            p2[0, i] = late[i]

    @pl.when(last)
    def _():
        for i in range(27):
            p2[5, i] = p2[4, i]

    def finish_layer(x, carry):
        g = gx[x + 1, 0:8, 0:128]
        for i in range(27):
            a, b, c = stencil[i]
            value = roll(roll(p2[x + 1 - a, i], b, 0), c, 1)[0:8, 0:128]
            value = jnp.where(value > limit, value, p2[x + 1, 26 - i, 0:8, 0:128])
            fine[i, x] = jnp.where(g > 0.0, value, 0.0)
        return carry

    lax.fori_loop(0, 4, finish_layer, 0)


def f32(*shape):
    return jax.ShapeDtypeStruct(shape, jnp.float32)


def call(kernel, name, out_shape, scratch, *args, held=0, cost=0):
    vmem = pl.BlockSpec(memory_space=pltpu.VMEM)
    raw = pl.BlockSpec(memory_space=pltpu.HBM)
    return pl.pallas_call(
        kernel,
        out_shape=out_shape,
        in_specs=[pl.BlockSpec(memory_space=pltpu.SMEM)] + [raw] * held + [vmem] * (len(args) - 1 - held),
        out_specs=[vmem] * len(out_shape),
        scratch_shapes=[pltpu.VMEM(s, jnp.float32) for s in scratch]
        + ([pltpu.SemaphoreType.DMA((held,))] if held else []),
        compiler_params=pltpu.CompilerParams(vmem_limit_bytes=40 * 1024 * 1024),
        cost_estimate=pl.CostEstimate(flops=cost, bytes_accessed=1, transcendentals=0) if cost else None,
        name=name,
    )(*args)


def body(pop, cpop, mask, inflow, part_dest, part_cell, part_vel, part_frac, part_drag):
    gx, gy, h, gz = [lax.axis_index(a) for a in ("gx", "y", "h", "gz")]
    n_gx, n_y, n_gz = lax.axis_size("gx"), lax.axis_size("y"), lax.axis_size("gz")
    row = gy * 2 + h
    sc = jnp.stack(
        [
            h,
            gx % 2,
            gz % 2,
            (gx == 0).astype(jnp.int32),
            (gx == n_gx - 1).astype(jnp.int32),
            (row > 0).astype(jnp.int32),
            (row < 2 * n_y - 1).astype(jnp.int32),
            (gz > 0).astype(jnp.int32),
            (gz < n_gz - 1).astype(jnp.int32),
        ]
    ).astype(jnp.int32)
    faces, vel, cc, r127, rs = call(
        pack_kernel,
        "pack",
        [
            f32(2, T_FACE, 8, 128),
            f32(3, 4, 8, 128),
            f32(8, 27, 8, 128),
            f32(27, 8, 128),
            f32(9, 8, 128),
        ],
        [(27, 8, 8, 128), (4, 4, 8, 128)],
        sc,
        pop,
        cpop,
        mask,
        inflow,
    )
    (outbox,) = call(
        route_kernel,
        "route",
        [f32(64, 128)],
        [],
        sc,
        part_dest.reshape(1, 256),
        part_cell.reshape(1, 256),
        part_vel,
        part_frac,
        part_drag.reshape(1, 256),
        rs,
        cost=50_000_000_000,
    )
    last = n_gx - 1
    spot = lambda x, y, z: (x * n_y + y) * 2 + z
    far_ends = [(spot(a, y, 1), spot(b, y + 1, 0)) for a, b in ((0, last), (last, 0)) for y in range(n_y - 1)]
    corner = lax.ppermute(
        faces[1, T_LEVEL:T_FACE], ("gx", "y", "h"), far_ends + [(j, i) for i, j in far_ends]
    )
    near = lax.ppermute(faces, "h", [(0, 1), (1, 0)])
    arr = lax.all_to_all(outbox.reshape(2 * n_gx, 2, 128), ("gx", "h"), 0, 0, tiled=True)
    near_ends = [(2 * last + 1, 0), (2 * last, 1)]
    ends = lax.ppermute(
        jnp.concatenate(
            [near[0, T_LEVEL:T_FACE], near[1, T_LEVEL:T_FACE], faces[0, T_LEVEL:T_FACE]], axis=0
        ),
        ("gx", "h"),
        near_ends + [(j, i) for i, j in near_ends],
    )
    onward = [(2 * y, 2 * y + 2) for y in range(n_y - 1)]
    onward += [(2 * y + 3, 2 * y + 1) for y in range(n_y - 1)]
    partner = jnp.where(h == 0, arr[1::2], arr[0::2]).reshape(4, 8, 128)
    fwd = lax.ppermute(near[1], ("y", "h"), onward)
    partner, _ = lax.optimization_barrier((partner, near))
    third = lax.ppermute(partner, ("y", "h"), onward)
    ye, xb, xa, ccy = call(
        deposit_kernel,
        "deposit",
        [f32(4, 31, 16, 128), f32(T_X, 8, 128), f32(T_X, 8, 128), f32(8, 27, 8, 128)],
        [(T_FACE, 8, 128), (T_FACE, 8, 128)],
        sc,
        pop,
        mask,
        vel,
        cc,
        near,
        fwd,
        arr,
        third,
        corner,
        ends,
        cost=50_000_000_000,
    )
    inner = [(i, i + 1) for i in range(1, n_gx - 1, 2)]
    xbr = lax.ppermute(xb, "gx", inner + [(j, i) for i, j in inner])
    xar = lax.ppermute(xa, "gx", [(i, i ^ 1) for i in range(n_gx)])
    za, zb, swr, sw, inf = call(
        column_kernel,
        "columns",
        [f32(8, 8, 128), f32(8, 8, 128), f32(T_SW, 8, 128), f32(5, 8, 128), f32(8, 128)],
        [],
        sc,
        ye,
        xbr,
        xar,
        ccy,
        rs,
        inflow,
        near,
        fwd,
        ends,
        corner,
    )
    zar = lax.ppermute(za, "gz", [(i, i ^ 1) for i in range(n_gz)])
    inner = [(i, i + 1) for i in range(1, n_gz - 1, 2)]
    zbr = lax.ppermute(zb, "gz", inner + [(j, i) for i, j in inner])
    fine, coarse = call(
        step_kernel,
        "steps",
        [f32(27, 4, 8, 128), f32(27, 8, 4, 64)],
        [
            (8, 27, 16, 256),
            (6, 27, 16, 256),
            (6, 16, 256),
            (6, 3, 16, 256),
            (10, 27, 8, 128),
            (3, 27, 8, 128),
            (27, 16, 256),
        ],
        sc,
        ye,
        xbr,
        xar,
        swr,
        ccy,
        sw,
        inf,
        zar,
        zbr,
    )
    return fine, coarse


def solution(mesh):
    n_gx, n_gy, n_gz = [mesh.shape[a] for a in ("gx", "gy", "gz")]
    split = Mesh(mesh.devices.reshape(n_gx, n_gy // 2, 2, n_gz), ("gx", "y", "h", "gz"))
    gy = ("y", "h")
    return jax.shard_map(
        body,
        mesh=split,
        in_specs=(
            P(None, "gx", gy, "gz"),
            P(None, "gx", gy, "gz"),
            P("gx", gy, "gz"),
            P(gy, "gz"),
            P("gx", gy, "gz", None, None),
            P("gx", gy, "gz", None),
            P("gx", gy, "gz", None, None),
            P("gx", gy, "gz", None, None),
            P("gx", gy, "gz", None),
        ),
        out_specs=(P(None, "gx", gy, "gz"), P(None, "gx", gy, "gz")),
        check_vma=False,
    )
```

```python
import jax
import jax.numpy as jnp
from jax import lax
from jax.experimental import pallas as pl
from jax.experimental.pallas import tpu as pltpu
from jax.sharding import Mesh, PartitionSpec as P

tau_fine = 1.3
tau_coarse = 0.9
prolong_factor = (tau_fine - 1.0) / (2.0 * tau_coarse)
restrict_factor = 2.0 * (tau_coarse - 1.0) / tau_fine
stencil = [(a, b, c) for a in (-1, 0, 1) for b in (-1, 0, 1) for c in (-1, 0, 1)]
class_weight = (8.0 / 27.0, 2.0 / 27.0, 1.0 / 54.0, 1.0 / 216.0)
wall = -1e30
limit = -1e29


def moving(axis, way):
    return [i for i in range(27) if stencil[i][axis] == way]


UP = [moving(axis, 1) for axis in range(3)]
DOWN = [moving(axis, -1) for axis in range(3)]

T_DEEP, T_COARSE, T_LEVEL, T_FACE = 14, 23, 22, 33
X_ROWS, X_COARSE, T_X = 40, 60, 69


def level_rows():
    rows = [(ch, 0) for ch in range(46)] + [(ch, 1) for ch in range(45)]
    spots = [(22, r, 64 * half) for r in range(4, 8) for half in range(2)]
    spots += [(27, r, 64) for r in range(8)]
    spots += [(t, r, 64 * half) for t in range(28, 33) for r in range(8) for half in range(2)]
    return dict(zip(rows, spots))


LEVEL = level_rows()
T_SW = 18

z_items = [(0, x, ch) for x in range(1, 7) for ch in range(31)]
z_items += [(0, 0, i) for i in UP[0]] + [(0, 7, i) for i in DOWN[0]]
z_deep = [(1, x, j) for x in range(1, 7) for j in range(9)]


def z_layout(way):
    inward = UP[2] if way > 0 else DOWN[2]
    items = list(z_items) + [(1, x, inward[j]) for (_, x, j) in z_deep]
    items += [(1, 0, i) for i in inward if stencil[i][0] == 1]
    items += [(1, 7, i) for i in inward if stencil[i][0] == -1]
    return {item: spot for spot, item in enumerate(items)}


def c_layout(way):
    inward = UP[2] if way > 0 else DOWN[2]
    items = [("c", x, i) for x in range(1, 9) for i in inward]
    items += [("c", 0, i) for i in inward if stencil[i][0] == 1]
    items += [("c", 9, i) for i in inward if stencil[i][0] == -1]
    items += [("g", ch, 0) for ch in range(45)] + [("g", ch, 1) for ch in range(27)]
    items += [("g", 27 + j, 1) for j in range(9) if stencil[UP[0][j]][2] == way]
    items += [("g", 36 + j, 1) for j in range(9) if stencil[DOWN[0][j]][2] == way]
    items += [("i",)]
    return {item: spot for spot, item in enumerate(items)}


ZL = {1: z_layout(1), -1: z_layout(-1)}
CL = {1: c_layout(1), -1: c_layout(-1)}


def roll(value, by, axis):
    by = by % value.shape[axis]
    return value if by == 0 else pltpu.roll(value, by, axis)


def iota(shape, axis):
    return lax.broadcasted_iota(jnp.int32, shape, axis)


def dot(a, b, contract=(1, 0)):
    return lax.dot_general(
        a,
        b,
        (((contract[0],), (contract[1],)), ((), ())),
        precision=lax.Precision.HIGHEST,
        preferred_element_type=jnp.float32,
    )


def select(value, pick, left=False):
    total = None
    pick = pick.astype(jnp.bfloat16)
    for _ in range(3):
        part = value.astype(jnp.bfloat16)
        value = value - part.astype(jnp.float32)
        a, b = (pick, part) if left else (part, pick)
        product = jnp.dot(a, b, preferred_element_type=jnp.float32)
        total = product if total is None else total + product
    return total


def moments(n):
    totals = [n[13], None, None, None]
    parts = [[None] * 4 for _ in range(3)]
    for i in range(14, 27):
        c = stencil[i]
        k = abs(c[0]) + abs(c[1]) + abs(c[2])
        both, odd = n[i] + n[26 - i], n[i] - n[26 - i]
        totals[k] = both if totals[k] is None else totals[k] + both
        for axis in range(3):
            if c[axis]:
                have = parts[axis][k]
                if have is None:
                    parts[axis][k] = odd if c[axis] > 0 else -odd
                else:
                    parts[axis][k] = have + odd if c[axis] > 0 else have - odd
    density = sum(class_weight[k] * totals[k] for k in range(4))
    momentum = [sum(class_weight[k] * parts[axis][k] for k in (1, 2, 3)) for axis in range(3)]
    return density, momentum


def equilibrium(s, u):
    base = s - (1.5 * (u[0] * u[0] + u[1] * u[1] + u[2] * u[2])) * s
    s3, s45 = 3.0 * s, 4.5 * s
    out = [None] * 27
    out[13] = base
    for i in range(14, 27):
        cu = None
        for axis in range(3):
            c = stencil[i][axis]
            if c:
                if cu is None:
                    cu = u[axis] if c > 0 else -u[axis]
                else:
                    cu = cu + u[axis] if c > 0 else cu - u[axis]
        even, odd = base + s45 * (cu * cu), s3 * cu
        out[i], out[26 - i] = even + odd, even - odd
    return out


def collide(n, g, force, tau):
    density, m = moments(n)
    s = jnp.where(density == 0.0, 1.0, density) if g is None else density + (1.0 - g)
    inverse = 1.0 / s
    if force is not None:
        m = [m[k] + tau * force[k] for k in range(3)]
    e = equilibrium(s * (1.0 / tau), [v * inverse for v in m])
    post = [(1.0 - 1.0 / tau) * n[i] + e[i] for i in range(27)]
    return post if g is None else [jnp.where(g > 0.0, p, wall) for p in post]


def interface(n, factor):
    density, m = moments(n)
    density = jnp.where(density == 0.0, 1.0, density)
    inverse = 1.0 / density
    e = equilibrium(density, [v * inverse for v in m])
    return [e[i] + factor * (n[i] - e[i]) for i in range(27)]


S_H, S_CORE, S_ODD, S_FIRST, S_LAST, S_YLO, S_YHI, S_ZLO, S_ZHI = range(9)


def route_kernel(sc, pdest, pcell, pvel, pfrac, pdrag, anchor, outbox):
    del sc, anchor
    dest = pdest[...]
    onehot = (iota((16, 256), 0) == dest).astype(jnp.float32)
    earlier = (iota((256, 256), 0) < iota((256, 256), 1)).astype(jnp.bfloat16)
    before = jnp.dot(onehot.astype(jnp.bfloat16), earlier, preferred_element_type=jnp.float32)
    rank = jnp.sum(onehot * before, axis=0, keepdims=True).astype(jnp.int32)
    slot = (iota((32, 256), 0) == rank).astype(jnp.float32)
    row = iota((64, 256), 0)
    hit = (row >> 2) == dest
    odd = (row & 1) == 1
    fields = [pvel[0, 0, 0, k : k + 1, :] for k in range(3)] + [pdrag[...]]
    fields += [pfrac[0, 0, 0, k : k + 1, :] for k in range(3)] + [pcell[...].astype(jnp.float32)]
    for q in range(4):
        values = jnp.where(hit, jnp.where(odd, fields[4 + q], fields[q]), 0.0)
        outbox[:, 32 * q : 32 * q + 32] = dot(values, slot, (1, 1))


def pack_kernel(
    sc, pop, cpop, mask, inflow, faces, vel, cc, r127, rs, rc, mom,
):
    h = sc[S_H]
    rc[...] = jnp.zeros(rc.shape, jnp.float32)
    faces[...] = jnp.zeros(faces.shape, jnp.float32)
    for x in range(4):
        density, m = moments([pop[i, x] for i in range(27)])
        inverse = 1.0 / (density + (1.0 - mask[x].astype(jnp.float32)))
        mom[0, x] = density
        for k in range(3):
            mom[k + 1, x] = m[k]
            vel[k, x] = m[k] * inverse
    for i in range(27):
        rc[i, :, 0:4, 0:64] = cpop[i]
        r127[i] = rc[i, 7]
    for x in range(8):
        post = collide([rc[i, x] for i in range(27)], None, None, tau_coarse)
        for i in range(27):
            cc[x, i] = post[i]
    pair = jnp.concatenate([pop[i, 0] + pop[i, 1] for i in range(27)], axis=0)
    narrow = ((iota((128, 128), 0) >> 1) == iota((128, 128), 1)).astype(jnp.float32)
    down, across = iota((216, 216), 0), iota((216, 216), 1)
    low = ((down >> 3) == (across >> 3)) & (((across & 7) >> 1) == (down & 7))
    mean = 0.125 * select(select(pair, narrow), low.astype(jnp.float32), left=True)
    settled = interface([mean[8 * i : 8 * i + 8] for i in range(27)], restrict_factor)
    for j in range(9):
        rs[j] = settled[DOWN[0][j]]
    for way in (1, -1):
        face = h if way > 0 else 1 - h
        depths, coarse_depths = ((7, 6, 5), (3, 2)) if way > 0 else ((0, 1, 2), (0, 1))
        inward = UP[1] if way > 0 else DOWN[1]
        for x in range(4):

            def put(base, k, ref, depth):
                at = 4 * (k % 2) + x
                value = ref[depth : depth + 1, :].astype(jnp.float32)
                faces[face, base + k // 2, at : at + 1, :] = value

            for ch in range(27):
                put(0, ch, pop.at[ch, x], depths[0])
            put(0, 27, mask.at[x], depths[0])
            for k in range(9):
                put(T_DEEP, k, pop.at[inward[k], x], depths[1])
            for k in range(4):
                put(T_DEEP, 9 + k, mom.at[k, x], depths[1])
            put(T_DEEP, 13, mask.at[x], depths[1])
            for k in range(3):
                put(T_DEEP, 14 + k, vel.at[k, x], depths[2])
        r = coarse_depths[0]
        for j, i in enumerate(inward):
            lane = 64 * (j // 5)
            for x in range(8):
                faces[face, T_COARSE + j % 5, x : x + 1, lane : lane + 64] = cc[x, i, r : r + 1, 0:64]
        for (ch, depth), (tile, at, lane) in LEVEL.items():
            r = coarse_depths[depth]
            if ch < 27:
                value = rc[ch, 7, r : r + 1, 0:64]
            elif ch < 36:
                value = cc[6, UP[0][ch - 27], r : r + 1, 0:64]
            elif ch < 45:
                value = rs[ch - 36, r : r + 1, 0:64]
            else:
                value = inflow[r : r + 1, :]
            faces[face, tile, at : at + 1, lane : lane + 64] = value


def particle_fields(rows):
    lane = iota((2, 128), 1) >> 5
    chunks = [[] for _ in range(4)]
    for k in range(4):
        turned = [[roll(rows[4 * k + j], 32 * s, 1) for s in range(4)] for j in range(4)]
        for q in range(4):
            value = turned[0][(0 - q) % 4]
            for j in range(1, 4):
                value = jnp.where(lane == j, turned[j][(j - q) % 4], value)
            chunks[q].append(value)
    flat = [jnp.concatenate(chunks[q], axis=1) for q in range(4)]
    return [flat[f % 4][f // 4 : f // 4 + 1, :] for f in range(8)]


def deposit(fields, velocity, xr, yr, keep):
    rows = velocity[0].shape[0]
    count = fields[0].shape[1]
    cell = fields[7].astype(jnp.int32)
    ix, iy, iz = cell >> 10, (cell >> 7) & 7, cell & 127
    fx, fy, fz = fields[4:7]
    lane = iota((128, count), 0)
    along = jnp.where(lane == iz, 1.0 - fz, jnp.where(lane == iz + 1, fz, 0.0))
    across = jnp.where(xr == ix, 1.0 - fx, jnp.where(xr == ix + 1, fx, 0.0))
    across = across * jnp.where(yr == iy, 1.0 - fy, jnp.where(yr == iy + 1, fy, 0.0))
    seen = dot(jnp.concatenate(velocity, axis=0), along)
    pushes = []
    for k in range(3):
        sampled = jnp.sum(seen[k * rows : (k + 1) * rows] * across, axis=0, keepdims=True)
        impulse = fields[3] * (fields[k] - sampled)
        pushes.append(impulse * across[0:keep])
    force = dot(jnp.concatenate(pushes, axis=0), along, (1, 1))
    return [force[k * keep : (k + 1) * keep] for k in range(3)]


def choose(sc, near, fwd):
    lower = sc[S_H] == 0
    return (lambda t: jnp.where(lower, near[0, t], fwd[t])), (lambda t: jnp.where(lower, fwd[t], near[0, t]))


def deposit_kernel(sc, pop, mask, vel, cc, near, fwd, arr, third_in, corner, ends, ye, xb, xa, ccy, hi, lo):
    del corner, ends
    h = sc[S_H]
    lower = h == 0
    up, down = choose(sc, near, fwd)
    for t in range(T_FACE):
        hi[t], lo[t] = up(t), down(t)
    own = particle_fields([arr[2 * s + h] for s in range(16)])
    partner = particle_fields([arr[2 * s + 1 - h] for s in range(16)])
    third = particle_fields([third_in[s // 4, 2 * (s % 4) : 2 * (s % 4) + 2, :] for s in range(16)])
    high = [jnp.where(lower, a, b) for a, b in zip(partner, third)]
    low = [jnp.where(lower, b, a) for a, b in zip(partner, third)]
    rows32 = iota((32, 1), 0)
    force = deposit(
        own,
        [jnp.concatenate([vel[k, x] for x in range(4)], axis=0) for k in range(3)],
        rows32 >> 3,
        rows32 & 7,
        32,
    )
    row = iota((8, 128), 0)
    first_half = row < 4

    def layer(base, k):
        a, b = hi[base + k // 2], lo[base + k // 2]
        return jnp.where(first_half, roll(a, 4, 0), b) if k % 2 else jnp.where(first_half, a, roll(b, 4, 0))

    n1 = [layer(0, ch) for ch in range(27)]
    g1 = layer(0, 27)
    n2 = [layer(T_DEEP, k) for k in range(9)]
    density2, m2, g2 = layer(T_DEEP, 9), [layer(T_DEEP, 10 + k) for k in range(3)], layer(T_DEEP, 13)
    v3 = [layer(T_DEEP, 14 + k) for k in range(3)]
    density1, m1 = moments(n1)
    inverse1, inverse2 = 1.0 / (density1 + (1.0 - g1)), 1.0 / (density2 + (1.0 - g2))
    rows16 = iota((16, 1), 0)
    pushed = []
    for above, fields in ((True, high), (False, low)):
        velocity = []
        for k in range(3):
            a, b = m1[k] * inverse1, m2[k] * inverse2
            c = jnp.where(first_half, v3[k] if above else roll(v3[k], 4, 0), 0.0)
            ab = jnp.where(first_half, a, roll(b, 4, 0)) if above else jnp.where(first_half, roll(a, 4, 0), b)
            velocity.append(jnp.concatenate([ab, c], axis=0))
        depth = rows16 >> 2
        pushed.append(deposit(fields, velocity, rows16 & 3, depth if above else 7 - depth, 8))
    f1 = [jnp.where(first_half, a, roll(b, 4, 0)) for a, b in zip(*pushed)]
    f2 = [jnp.where(first_half, roll(a, 4, 0), b) for a, b in zip(*pushed)]
    side1 = collide(n1, g1, f1, tau_fine) + [g1] + f1
    s2 = density2 + (1.0 - g2)
    u2 = [(m2[k] + tau_fine * f2[k]) * inverse2 for k in range(3)]
    u2[1] = jnp.where(first_half, u2[1], -u2[1])
    e2 = equilibrium(s2 * (1.0 / tau_fine), u2)
    side2 = [
        jnp.where(g2 > 0.0, (1.0 - 1.0 / tau_fine) * n2[k] + e2[DOWN[1][k]], wall) for k in range(9)
    ]
    for x in range(4):
        g = mask[x].astype(jnp.float32)
        f = [force[k][8 * x : 8 * x + 8] for k in range(3)]
        mine = collide([pop[i, x] for i in range(27)], g, f, tau_fine) + [g] + f
        for ch in range(31):
            ye[x, ch, 0:8, :] = mine[ch]
            value = jnp.where(row == 0, roll(side1[ch], -x, 0), 0.0)
            value = jnp.where(row == 7, roll(side1[ch], 3 - x, 0), value)
            if ch in DOWN[1]:
                value = jnp.where(row == 1, roll(side2[DOWN[1].index(ch)], 1 - x, 0), value)
            if ch in UP[1]:
                value = jnp.where(row == 6, roll(side2[UP[1].index(ch)], 2 - x, 0), value)
            ye[x, ch, 8:16, :] = value
    ccy[...] = cc[...]
    has_hi, has_lo = sc[S_YHI] == 1, sc[S_YLO] == 1
    for face, way, has, r in ((hi, DOWN[1], has_hi, 4), (lo, UP[1], has_lo, 7)):
        for j, i in enumerate(way):
            lane = 64 * (j // 5)
            for x in range(8):
                value = face[T_COARSE + j % 5, x : x + 1, lane : lane + 64]
                ccy[x, i, r : r + 1, 0:64] = jnp.where(has, value, wall)
    even = sc[S_CORE] == 0
    outer = (row < 2) | (row >= 6)

    def send(t, a, b):
        xa[t], xb[t] = jnp.where(even, a, b), jnp.where(even, b, a)

    ups = [(3, ch) for ch in range(31)] + [(2, i) for i in UP[0]]
    downs = [(0, ch) for ch in range(31)] + [(1, i) for i in DOWN[0]]
    for k in range(40):
        send(k, ye[ups[k] + (slice(0, 8),)], ye[downs[k] + (slice(0, 8),)])
    for k in range(20):
        pairs = []
        for which in (ups, downs):
            first, second = which[2 * k], which[2 * k + 1]
            value = roll(ye[second + (slice(8, 16),)], 4, 0)
            pairs.append(jnp.where(outer, ye[first + (slice(8, 16),)], value))
        send(X_ROWS + k, *pairs)
    for j in range(9):
        send(X_COARSE + j, ccy[7, UP[0][j]], ccy[0, DOWN[0][j]])


def x_tile(ye, up, down, x, ch):
    if 2 <= x <= 5:
        return ye[x - 2, ch]
    face = down if x < 2 else up
    slot = ch if x in (1, 6) else 31 + (UP[0] if x == 0 else DOWN[0]).index(ch)
    row = iota((8, 128), 0)
    rest = roll(face(X_ROWS + slot // 2), 4 * (slot % 2), 0)
    return jnp.concatenate([face(slot), jnp.where((row < 2) | (row >= 6), rest, 0.0)], axis=0)


def pick(sc, index, a, b):
    even = sc[index] == 0
    return (lambda t: jnp.where(even, a[t], b[t])), (lambda t: jnp.where(even, b[t], a[t]))


def level_layers(sc, rs, inflow, near, fwd, ends, corner, swr, sw, inf):
    wide = T_FACE - T_LEVEL
    for h in range(2):
        here, there, other, beyond = ((3, 2), (0, 1), (4, 5), (7, 6)) if h == 0 else ((0, 1), (3, 2), (7, 6), (4, 5))

        def put(ch, source, base, rows, ref, to):
            for depth in range(2):
                if (ch, depth) in LEVEL:
                    tile, at, lane = LEVEL[ch, depth]
                    r = rows[depth]
                    ref[r : r + 1, to : to + 64] = source[tile + base, at : at + 1, lane : lane + 64]

        def received(channels):
            for q, ch in enumerate(channels):
                ref, to = swr.at[q // 2], 64 * (q % 2)
                put(ch, ends, -T_LEVEL, here, ref, to)
                put(ch, ends, wide - T_LEVEL, there, ref, to)
                put(ch, ends, 2 * wide - T_LEVEL, other, ref, to)
                put(ch, corner, -T_LEVEL, beyond, ref, to)

        @pl.when((sc[S_FIRST] == 1) & (sc[S_H] == h))
        def _():
            received(range(36))
            for j in range(9):
                ref, to = sw.at[j // 2], 64 * (j % 2)
                ref[0:4, to : to + 64] = rs[j, 0:4, 0:64]
                put(36 + j, near.at[0], 0, other, ref, to)
                put(36 + j, fwd, 0, beyond, ref, to)
            inf[0:4, 0:64] = inflow[...]
            put(45, near.at[0], 0, other, inf, 0)
            put(45, fwd, 0, beyond, inf, 0)

        @pl.when((sc[S_LAST] == 1) & (sc[S_H] == h))
        def _():
            received(range(36, 45))


def column_kernel(
    sc, ye, xbr, xar, ccy, rs, inflow, near, fwd, ends, corner, za, zb, swr, sw, inf
):
    level_layers(sc, rs, inflow, near, fwd, ends, corner, swr, sw, inf)
    up, down = pick(sc, S_CORE, xar, xbr)
    lane = iota((16, 128), 1)
    lane8 = iota((8, 128), 1)
    made = {}
    for way in (1, -1):
        tiles = [jnp.zeros((16, 128), jnp.float32) for _ in range(3)]
        for (depth, x, ch), spot in ZL[way].items():
            source = 127 - depth if way > 0 else depth
            value = roll(x_tile(ye, up, down, x, ch), spot - source, 1)
            tiles[spot // 128] = jnp.where(lane == spot % 128, value, tiles[spot // 128])
        out = [t[8 * k : 8 * k + 8] for t in tiles for k in range(2)]
        tiles = [jnp.zeros((8, 128), jnp.float32) for _ in range(2)]
        for item, spot in CL[way].items():
            if item[0] == "c":
                _, x, i = item
                if x == 0:
                    value = down(X_COARSE + UP[0].index(i))
                elif x == 9:
                    value = up(X_COARSE + DOWN[0].index(i))
                else:
                    value = ccy[x - 1, i]
                source = 63 if way > 0 else 0
            elif item[0] == "g":
                _, ch, depth = item
                q = ch if ch < 36 else ch - 36
                value = swr[q // 2] if ch < 36 else sw[q // 2]
                source = (63 - depth if way > 0 else depth) + 64 * (q % 2)
            else:
                value = inf[...]
                source = 63 if way > 0 else 0
            value = roll(value, spot - source, 1)
            tiles[spot // 128] = jnp.where(lane8 == spot % 128, value, tiles[spot // 128])
        made[way] = out + tiles
    even = sc[S_ODD] == 0
    for t in range(8):
        za[t] = jnp.where(even, made[1][t], made[-1][t])
        zb[t] = jnp.where(even, made[-1][t], made[1][t])


def step_kernel(
    sc, ye, xbr, xar, swr, ccy, sw, inf, zar, zbr, fine, coarse, p1, p2, gx, fx, ce, gr, late
):
    up, down = pick(sc, S_CORE, xar, xbr)
    zup, zdown = pick(sc, S_ODD, zar, zbr)
    has_yhi, has_ylo, has_zhi, has_zlo = [sc[k] == 1 for k in (S_YHI, S_YLO, S_ZHI, S_ZLO)]
    first, last = sc[S_FIRST] == 1, sc[S_LAST] == 1
    fz_up = [jnp.concatenate([zup(2 * k), zup(2 * k + 1)], axis=0) for k in range(3)]
    fz_down = [jnp.concatenate([zdown(2 * k), zdown(2 * k + 1)], axis=0) for k in range(3)]
    cz_up, cz_down = [zup(6), zup(7)], [zdown(6), zdown(7)]
    lane = iota((16, 128), 1)
    lane8 = iota((8, 128), 1)

    def side(x, ch):
        blank = wall if ch < 27 else 0.0
        value = jnp.zeros((16, 128), jnp.float32)
        for depth in range(2):
            for way, source, has, at in ((-1, fz_up, has_zhi, depth), (1, fz_down, has_zlo, 127 - depth)):
                spot = ZL[way].get((depth, x, ch))
                if spot is not None:
                    moved = jnp.where(has, roll(source[spot // 128], at - spot, 1), blank)
                    value = jnp.where(lane == at, moved, value)
        return value

    for x in range(8):
        for ch in range(31) if 0 < x < 7 else (UP[0] if x == 0 else DOWN[0]):
            main, rest = x_tile(ye, up, down, x, ch), side(x, ch)
            if ch < 27:
                to = p1.at[x, ch]
            elif ch == 27:
                to = gx.at[x - 1]
            else:
                to = fx.at[x - 1, ch - 28]
            to[:, 0:128] = main
            to[:, 128:256] = rest

    row8 = iota((8, 128), 0)
    inside = (row8 < 4) | ((row8 < 6) & has_yhi) | ((row8 >= 6) & has_ylo)
    inside = inside & (
        (lane8 < 64) | ((lane8 >= 64) & (lane8 < 66) & has_zhi) | ((lane8 >= 126) & has_zlo)
    )

    def c_side(value, up_item, down_item, blank, at=64, end=127):
        for way, source, has, item, to in ((-1, cz_up, has_zhi, up_item, at), (1, cz_down, has_zlo, down_item, end)):
            spot = CL[way].get(item)
            if spot is not None:
                moved = jnp.where(has, roll(source[spot // 128], to - spot, 1), blank)
                value = jnp.where(lane8 == to, moved, value)
        return value

    def ghost(ch, ref, q):
        value = roll(ref[q // 2], 64 * (q % 2), 1)
        value = jnp.where(lane8 < 64, value, 0.0)
        for depth in range(2):
            item = ("g", ch, depth)
            value = c_side(value, item, item, 0.0, 64 + depth, 127 - depth)
        return value

    for x in range(8):
        for i in range(27):
            ce[x + 1, i] = c_side(ccy[x, i], ("c", x + 1, i), ("c", x + 1, i), wall)
    inflow = c_side(inf[...], ("i",), ("i",), 0.0)
    zero = jnp.zeros((8, 128), jnp.float32)
    inlet = equilibrium(jnp.ones((8, 128), jnp.float32), [inflow, zero, zero])
    for j in range(9):
        i = UP[0][j]
        came = c_side(down(X_COARSE + j), ("c", 0, i), ("c", 0, i), wall)
        ce[0, i] = jnp.where(first, jnp.where(inside, inlet[i], wall), came)
        i = DOWN[0][j]
        came = c_side(up(X_COARSE + j), ("c", 9, i), ("c", 9, i), wall)
        ce[9, i] = jnp.where(last, jnp.where(inside, ghost(j, swr, j), wall), came)
    for i in range(27):
        a, b, c = stencil[i]
        for x in range(8):
            value = roll(roll(ce[x + 1 - a, i], b, 0), c, 1)
            value = jnp.where(value > limit, value, ce[x + 1, 26 - i])
            coarse[i, x] = value[0:4, 0:64]

    @pl.when(first)
    def _():
        n127 = [ghost(i, swr, i) for i in range(27)]
        post = collide(n127, None, None, tau_coarse)
        for i in range(27):
            gr[1, i] = jnp.where(inside, post[i], wall)
        for j in range(9):
            gr[0, UP[0][j]] = jnp.where(inside, ghost(27 + j, swr, 27 + j), wall)
            gr[2, DOWN[0][j]] = jnp.where(inside, ghost(36 + j, sw, j), wall)
        later = []
        for i in range(27):
            a, b, c = stencil[i]
            value = roll(roll(gr[1 - a, i], b, 0), c, 1)
            value = jnp.where(value > limit, value, gr[1, 26 - i])
            later.append(jnp.where(inside, 0.5 * (n127[i] + value), 0.0))
        wide = ((iota((128, 256), 1) >> 1) == iota((128, 256), 0)).astype(jnp.float32)
        tall = ((iota((432, 216), 0) >> 1) == iota((432, 216), 1)).astype(jnp.float32)
        row16, lane256 = iota((16, 256), 0), iota((16, 256), 1)
        within = (row16 < 8) | ((row16 < 12) & has_yhi) | ((row16 >= 12) & has_ylo)
        within = within & (
            (lane256 < 128) | ((lane256 < 132) & has_zhi) | ((lane256 >= 252) & has_zlo)
        )
        both = interface(n127, prolong_factor) + interface(later, prolong_factor)
        spread = select(jnp.concatenate(both, axis=0), wide)
        fines = select(jnp.concatenate([spread[0:216], spread[216:432]], axis=1), tall, left=True)
        for k, to in enumerate((p1.at[1], late)):
            for i in range(27):
                fine_layer = fines[16 * i : 16 * i + 16, 256 * k : 256 * k + 256]
                to[i] = jnp.where(within, fine_layer, wall)

    @pl.when(last)
    def _():
        for i in range(27):
            p1[6, i] = p1[5, i]

    def stream_layer(m, carry):
        g = gx[m]
        for i in range(27):
            a, b, c = stencil[i]
            value = roll(roll(p1[m + 1 - a, i], b, 0), c, 1)
            value = jnp.where(value > limit, value, p1[m + 1, 26 - i])
            p2[m, i] = jnp.where(g > 0.0, value, 0.0)
        return carry

    lax.fori_loop(0, 6, stream_layer, 0)

    def collide_layer(m, carry):
        for y in range(2):
            for z in range(2):
                rows, lanes = slice(8 * y, 8 * y + 8), slice(128 * z, 128 * z + 128)
                post = collide(
                    [p2[m, i, rows, lanes] for i in range(27)],
                    gx[m, rows, lanes],
                    [fx[m, k, rows, lanes] for k in range(3)],
                    tau_fine,
                )
                for i in range(27):
                    p2[m, i, rows, lanes] = post[i]
        return carry

    lax.fori_loop(0, 6, collide_layer, 0)

    @pl.when(first)
    def _():
        for i in range(27):
            p2[0, i] = late[i]

    @pl.when(last)
    def _():
        for i in range(27):
            p2[5, i] = p2[4, i]

    def finish_layer(x, carry):
        g = gx[x + 1, 0:8, 0:128]
        for i in range(27):
            a, b, c = stencil[i]
            value = roll(roll(p2[x + 1 - a, i], b, 0), c, 1)[0:8, 0:128]
            value = jnp.where(value > limit, value, p2[x + 1, 26 - i, 0:8, 0:128])
            fine[i, x] = jnp.where(g > 0.0, value, 0.0)
        return carry

    lax.fori_loop(0, 4, finish_layer, 0)


def f32(*shape):
    return jax.ShapeDtypeStruct(shape, jnp.float32)


def call(kernel, name, out_shape, scratch, *args, held=0, cost=0):
    vmem = pl.BlockSpec(memory_space=pltpu.VMEM)
    raw = pl.BlockSpec(memory_space=pltpu.HBM)
    return pl.pallas_call(
        kernel,
        out_shape=out_shape,
        in_specs=[pl.BlockSpec(memory_space=pltpu.SMEM)] + [raw] * held + [vmem] * (len(args) - 1 - held),
        out_specs=[vmem] * len(out_shape),
        scratch_shapes=[pltpu.VMEM(s, jnp.float32) for s in scratch]
        + ([pltpu.SemaphoreType.DMA((held,))] if held else []),
        compiler_params=pltpu.CompilerParams(vmem_limit_bytes=40 * 1024 * 1024),
        cost_estimate=pl.CostEstimate(flops=cost, bytes_accessed=1, transcendentals=0) if cost else None,
        name=name,
    )(*args)


def body(pop, cpop, mask, inflow, part_dest, part_cell, part_vel, part_frac, part_drag):
    gx, gy, h, gz = [lax.axis_index(a) for a in ("gx", "y", "h", "gz")]
    n_gx, n_y, n_gz = lax.axis_size("gx"), lax.axis_size("y"), lax.axis_size("gz")
    row = gy * 2 + h
    sc = jnp.stack(
        [
            h,
            gx % 2,
            gz % 2,
            (gx == 0).astype(jnp.int32),
            (gx == n_gx - 1).astype(jnp.int32),
            (row > 0).astype(jnp.int32),
            (row < 2 * n_y - 1).astype(jnp.int32),
            (gz > 0).astype(jnp.int32),
            (gz < n_gz - 1).astype(jnp.int32),
        ]
    ).astype(jnp.int32)
    faces, vel, cc, r127, rs = call(
        pack_kernel,
        "pack",
        [
            f32(2, T_FACE, 8, 128),
            f32(3, 4, 8, 128),
            f32(8, 27, 8, 128),
            f32(27, 8, 128),
            f32(9, 8, 128),
        ],
        [(27, 8, 8, 128), (4, 4, 8, 128)],
        sc,
        pop,
        cpop,
        mask,
        inflow,
    )
    (outbox,) = call(
        route_kernel,
        "route",
        [f32(64, 128)],
        [],
        sc,
        part_dest.reshape(1, 256),
        part_cell.reshape(1, 256),
        part_vel,
        part_frac,
        part_drag.reshape(1, 256),
        rs,
        cost=50_000_000_000,
    )
    last = n_gx - 1
    spot = lambda x, y, z: (x * n_y + y) * 2 + z
    far_ends = [(spot(a, y, 1), spot(b, y + 1, 0)) for a, b in ((0, last), (last, 0)) for y in range(n_y - 1)]
    corner = lax.ppermute(
        faces[1, T_LEVEL:T_FACE], ("gx", "y", "h"), far_ends + [(j, i) for i, j in far_ends]
    )
    near = lax.ppermute(faces, "h", [(0, 1), (1, 0)])
    arr = lax.all_to_all(outbox.reshape(2 * n_gx, 2, 128), ("gx", "h"), 0, 0, tiled=True)
    near_ends = [(2 * last + 1, 0), (2 * last, 1)]
    ends = lax.ppermute(
        jnp.concatenate(
            [near[0, T_LEVEL:T_FACE], near[1, T_LEVEL:T_FACE], faces[0, T_LEVEL:T_FACE]], axis=0
        ),
        ("gx", "h"),
        near_ends + [(j, i) for i, j in near_ends],
    )
    onward = [(2 * y, 2 * y + 2) for y in range(n_y - 1)]
    onward += [(2 * y + 3, 2 * y + 1) for y in range(n_y - 1)]
    partner = jnp.where(h == 0, arr[1::2], arr[0::2]).reshape(4, 8, 128)
    fwd = lax.ppermute(near[1], ("y", "h"), onward)
    partner, _ = lax.optimization_barrier((partner, near))
    third = lax.ppermute(partner, ("y", "h"), onward)
    ye, xb, xa, ccy = call(
        deposit_kernel,
        "deposit",
        [f32(4, 31, 16, 128), f32(T_X, 8, 128), f32(T_X, 8, 128), f32(8, 27, 8, 128)],
        [(T_FACE, 8, 128), (T_FACE, 8, 128)],
        sc,
        pop,
        mask,
        vel,
        cc,
        near,
        fwd,
        arr,
        third,
        corner,
        ends,
        cost=50_000_000_000,
    )
    inner = [(i, i + 1) for i in range(1, n_gx - 1, 2)]
    xbr = lax.ppermute(xb, "gx", inner + [(j, i) for i, j in inner])
    xar = lax.ppermute(xa, "gx", [(i, i ^ 1) for i in range(n_gx)])
    za, zb, swr, sw, inf = call(
        column_kernel,
        "columns",
        [f32(8, 8, 128), f32(8, 8, 128), f32(T_SW, 8, 128), f32(5, 8, 128), f32(8, 128)],
        [],
        sc,
        ye,
        xbr,
        xar,
        ccy,
        rs,
        inflow,
        near,
        fwd,
        ends,
        corner,
    )
    zar = lax.ppermute(za, "gz", [(i, i ^ 1) for i in range(n_gz)])
    inner = [(i, i + 1) for i in range(1, n_gz - 1, 2)]
    zbr = lax.ppermute(zb, "gz", inner + [(j, i) for i, j in inner])
    fine, coarse = call(
        step_kernel,
        "steps",
        [f32(27, 4, 8, 128), f32(27, 8, 4, 64)],
        [
            (8, 27, 16, 256),
            (6, 27, 16, 256),
            (6, 16, 256),
            (6, 3, 16, 256),
            (10, 27, 8, 128),
            (3, 27, 8, 128),
            (27, 16, 256),
        ],
        sc,
        ye,
        xbr,
        xar,
        swr,
        ccy,
        sw,
        inf,
        zar,
        zbr,
    )
    return fine, coarse


def solution(mesh):
    n_gx, n_gy, n_gz = [mesh.shape[a] for a in ("gx", "gy", "gz")]
    split = Mesh(mesh.devices.reshape(n_gx, n_gy // 2, 2, n_gz), ("gx", "y", "h", "gz"))
    gy = ("y", "h")
    return jax.shard_map(
        body,
        mesh=split,
        in_specs=(
            P(None, "gx", gy, "gz"),
            P(None, "gx", gy, "gz"),
            P("gx", gy, "gz"),
            P(gy, "gz"),
            P("gx", gy, "gz", None, None),
            P("gx", gy, "gz", None),
            P("gx", gy, "gz", None, None),
            P("gx", gy, "gz", None, None),
            P("gx", gy, "gz", None),
        ),
        out_specs=(P(None, "gx", gy, "gz"), P(None, "gx", gy, "gz")),
        check_vma=False,
    )
```
